32 devices in a mesh: dp: 16 (over z, y, x), tensor: 2 (over core).
Axes of the slice: x: 2, y: 2, z: 4, core: 2. Of those that a mesh axis runs over, the one named last changes fastest.
Arguments:
- tokens: bfloat16 [512, 144, 384], P('dp', 'tensor'), may hold values from -6 to 6
- token_mask: int32 [512, 144], P('dp'), may hold values from 0 to 1, as said below
- shift_next: int32 [512], P('dp'), may hold values from 0 to 31, as said below
- cotangent: bfloat16 [512, 144, 384], P('dp', 'tensor'), may hold values from -6 to 6
- attend_gain: float32 [2, 384], replicated, may hold values from 0.1 to 1.9
- attend_shift: float32 [2, 384], replicated, may hold values from -1.5 to 1.5
- inward_weight: bfloat16 [2, 384, 3, 384], P(None, None, None, 'tensor'), may hold values from -0.3125 to 0.3125
- inward_bias: float32 [2, 2, 384], P(None, None, 'tensor'), may hold values from -1.5 to 1.5
- earth_bias: float32 [2, 12, 144, 144], P(None, 'tensor'), may hold values from -5 to 5
- outward_weight: bfloat16 [2, 384, 384], P(None, 'tensor'), may hold values from -0.875 to 0.875
- outward_bias: float32 [2, 384], replicated, may hold values from -1.5 to 1.5
- mixer_gain: float32 [2, 384], replicated, may hold values from 0.1 to 1.9
- mixer_shift: float32 [2, 384], replicated, may hold values from -1.5 to 1.5
- up_weight: bfloat16 [2, 384, 1536], P(None, None, 'tensor'), may hold values from -0.3125 to 0.3125
- up_bias: float32 [2, 1536], P(None, 'tensor'), may hold values from -1.5 to 1.5
- down_weight: bfloat16 [2, 1536, 384], P(None, 'tensor'), may hold values from -0.21875 to 0.21875
- down_bias: float32 [2, 384], replicated, may hold values from -1.5 to 1.5
Outputs:
- block_output: bfloat16 [512, 144, 384], P('dp', 'tensor')
- tokens_grad: bfloat16 [512, 144, 384], P('dp', 'tensor')
- attend_gain_grad: float32 [2, 384], replicated
- attend_shift_grad: float32 [2, 384], replicated
- inward_weight_grad: float32 [2, 384, 3, 384], P(None, None, None, 'tensor')
- inward_bias_grad: float32 [2, 2, 384], P(None, None, 'tensor')
- earth_bias_grad: float32 [2, 12, 144, 144], P(None, 'tensor')
- outward_weight_grad: float32 [2, 384, 384], P(None, 'tensor')
- outward_bias_grad: float32 [2, 384], replicated
- mixer_gain_grad: float32 [2, 384], replicated
- mixer_shift_grad: float32 [2, 384], replicated
- up_weight_grad: float32 [2, 384, 1536], P(None, None, 'tensor')
- up_bias_grad: float32 [2, 1536], P(None, 'tensor')
- down_weight_grad: float32 [2, 1536, 384], P(None, 'tensor')
- down_bias_grad: float32 [2, 384], replicated
The draws below stay inside these ranges and needn't reach their ends.
Inputs may be any that keep to these rules, and one draw needn't show every extreme that they name: `token_mask`: A window slot is live if it holds a valid token, dead if it holds none. Each device's 32 slots hold from 0 to 32 live windows, and some device holds 32; the live windows of all devices number exactly 16 times the devices of dp. The valid tokens of a live window are those of latitude row below some r (1 to 6) and longitude column below some c (1 to 12). `shift_next`: each device's 32 entries are a permutation of its slots 0 to 31: a live window goes to the next live window of its crop row on the same device, the last to the first, and a dead one to itself.
All inputs are finite; a program needn't handle non-finite values.
Results may differ from the reference program's by a relative error of at most 0.03.
Values may be sent and summed in bfloat16 or wider, within the bound.
No kernel may reach another device: no remote copies, remote signals or barrier semaphores. Data moves between devices by JAX's collectives and lax.ppermute only.
A program may use at most 256 MiB of HBM per device.

```python
import jax
import jax.numpy as jnp
from jax import lax

C = 384
HEADS = 12
FF = 1536
WIN = 144
BLOCKS = 2
RMAX = 16
HALF = 72
HOME = 32
PACKS = 512
N_DP = 16


def window_layout(key):
    devices = PACKS // HOME
    pair_key, excess_key, order_key, width_key, edge_key, row_key, col_key = jax.random.split(key, 7)
    pairing = jax.random.permutation(pair_key, devices)
    excess = jax.random.randint(excess_key, (devices // 2,), 0, RMAX)
    excess = excess.at[0].set(RMAX)
    live_counts = jnp.zeros((devices,), jnp.int32).at[pairing[0::2]].set(RMAX + excess).at[pairing[1::2]].set(RMAX - excess)
    slot_orders = jax.vmap(lambda sub_key: jax.random.permutation(sub_key, HOME))(jax.random.split(order_key, devices)).astype(jnp.int32)
    row_widths = jax.random.randint(width_key, (devices, 1), 2, 17)
    alive = slot_orders < live_counts[:, None]
    row_start = slot_orders // row_widths * row_widths
    row_length = jnp.maximum(jnp.minimum(row_widths, live_counts[:, None] - row_start), 1)
    following = row_start + (slot_orders - row_start + 1) % row_length
    slot_of_order = jnp.argsort(slot_orders, axis=1).astype(jnp.int32)
    successor = jnp.take_along_axis(slot_of_order, jnp.clip(following, 0, HOME - 1), axis=1)
    local_slots = jnp.broadcast_to(jnp.arange(HOME, dtype=jnp.int32)[None, :], (devices, HOME))
    east_next = jnp.where(alive, successor, local_slots).reshape(PACKS).astype(jnp.int32)
    edge_flag = jax.random.randint(edge_key, (devices, HOME), 0, 4) == 0
    lat_rows = jnp.where(edge_flag, jax.random.randint(row_key, (devices, HOME), 1, 7), 6)
    lon_cols = jnp.where(edge_flag, jax.random.randint(col_key, (devices, HOME), 1, 13), 12)
    token_index = jnp.arange(WIN, dtype=jnp.int32)
    lat_place = token_index % 36 // 6
    lon_place = 6 * (token_index // HALF) + token_index % 6
    valid = (lat_place[None, None, :] < lat_rows[:, :, None]) & (lon_place[None, None, :] < lon_cols[:, :, None]) & alive[:, :, None]
    return (valid.astype(jnp.int32).reshape(PACKS, WIN), east_next)


def draw_token_mask(key, part):
    valid, east_next = window_layout(key)
    return valid


def draw_shift_next(key, part):
    valid, east_next = window_layout(key)
    return east_next


def levels(rng, dims, cuts, low, top_value):
    level, own = 1.0, jax.random.fold_in(rng, 6)
    for axis_at, parts in cuts:
        draws = jnp.exp(jax.random.uniform(jax.random.fold_in(own, axis_at), (parts,), jnp.float32, low / len(cuts), top_value / len(cuts)))
        level = level * jnp.repeat(draws, dims[axis_at] // parts).reshape([-1 if axis == axis_at else 1 for axis in range(len(dims))])
    return level


def bell_draw(stream_key, extent, scale, reach, cuts=(), held_as=jnp.bfloat16):
    factor_of = levels(stream_key, extent, cuts, -0.22, 0.18) if cuts else 1.0
    array = jax.random.normal(stream_key, extent, jnp.float32) * scale * factor_of
    return jnp.minimum(jnp.maximum(array, -reach), reach).astype(held_as)


def setup_inputs(seed: int = 0) -> dict:
    key_list = jax.random.split(jax.random.key(seed), 18)
    tokens = bell_draw(key_list[0], (PACKS, WIN, C), 1.0, 6.0, ((0, 16), (1, 2)))
    token_mask = draw_token_mask(jax.random.fold_in(key_list[17], 71), 0)
    shift_next = draw_shift_next(jax.random.fold_in(key_list[17], 71), 0)
    cotangent = bell_draw(key_list[3], (PACKS, WIN, C), 1.0, 6.0, ((0, 16), (1, 2)))
    attend_gain = jnp.clip(1.0 + 0.18 * jax.random.normal(key_list[4], (BLOCKS, C), jnp.float32), 0.1, 1.9)
    attend_shift = bell_draw(key_list[5], (BLOCKS, C), 0.3, 1.5, (), jnp.float32)
    inward_weight = bell_draw(key_list[6], (BLOCKS, C, 3, C), C ** -0.5, 0.3125, ((3, 2),))
    inward_bias = bell_draw(key_list[7], (BLOCKS, 2, C), 0.3, 1.5, ((2, 2),), jnp.float32)
    earth_bias = bell_draw(key_list[8], (BLOCKS, HEADS, WIN, WIN), 1.0, 5.0, ((1, 2),), jnp.float32)
    outward_weight = bell_draw(key_list[9], (BLOCKS, C, C), (C // 8) ** -0.5, 0.875, ((1, 2),))
    outward_bias = bell_draw(key_list[10], (BLOCKS, C), 0.3, 1.5, (), jnp.float32)
    mixer_gain = jnp.clip(1.0 + 0.18 * jax.random.normal(key_list[11], (BLOCKS, C), jnp.float32), 0.1, 1.9)
    mixer_shift = bell_draw(key_list[12], (BLOCKS, C), 0.3, 1.5, (), jnp.float32)
    up_weight = bell_draw(key_list[13], (BLOCKS, C, FF), C ** -0.5, 0.3125, ((2, 2),))
    up_bias = bell_draw(key_list[14], (BLOCKS, FF), 0.3, 1.5, ((1, 2),), jnp.float32)
    down_weight = bell_draw(key_list[15], (BLOCKS, FF, C), (FF // 2) ** -0.5, 0.21875, ((1, 2),))
    down_bias = bell_draw(key_list[16], (BLOCKS, C), 0.3, 1.5, (), jnp.float32)
    return dict(tokens=tokens, token_mask=token_mask, shift_next=shift_next, cotangent=cotangent, attend_gain=attend_gain, attend_shift=attend_shift, inward_weight=inward_weight, inward_bias=inward_bias, earth_bias=earth_bias, outward_weight=outward_weight, outward_bias=outward_bias, mixer_gain=mixer_gain, mixer_shift=mixer_shift, up_weight=up_weight, up_bias=up_bias, down_weight=down_weight, down_bias=down_bias)


@jax.custom_vjp
def low(v):
    return lax.optimization_barrier(v.astype(jnp.bfloat16)).astype(jnp.float32)

@jax.custom_vjp
def low_back(v):
    return v

def low_keep(v):
    return (low(v), None)

def low_pass(kept, grad):
    return (grad,)

def back_keep(v):
    return (v, None)

def back_low(kept, grad):
    return (low(grad),)
low.defvjp(low_keep, low_pass)
low_back.defvjp(back_keep, back_low)

def layer_norm(values, gain, offset):
    centre = lax.optimization_barrier(jnp.mean(values, axis=-1, keepdims=True))
    centred = values - centre
    spread = lax.optimization_barrier(jnp.mean(centred * centred, axis=-1, keepdims=True))
    return centred * lax.rsqrt(spread + 1e-05) * gain + offset

def block(values, valid_tokens, params):
    gain_one, shift_one, inward, entry_bias, earth, outward, out_bias, gain_two, shift_two, up_proj, up_offset, down_proj, down_offset = params
    highest = lax.Precision.HIGHEST
    normed = low(layer_norm(values, gain_one, shift_one))
    projected = jnp.einsum('wtc,cjd->wtjd', normed, inward, precision=highest)
    query = low_back(low(projected[:, :, 0] + entry_bias[0]))
    keyed = low_back(low(projected[:, :, 1]))
    valued = low_back(low(projected[:, :, 2] + entry_bias[1]))
    window_count, token_count, feature_count = query.shape
    head_count = earth.shape[0]
    head_width = feature_count // head_count
    query_heads = query.reshape(window_count, token_count, head_count, head_width)
    key_heads = keyed.reshape(window_count, token_count, head_count, head_width)
    value_heads = valued.reshape(window_count, token_count, head_count, head_width)
    scores = jnp.einsum('wqhd,wkhd->whqk', query_heads, key_heads, precision=highest) * head_width ** (-0.5) + earth[None]
    scores = low_back(scores)
    scores = jnp.where(valid_tokens[:, None, None, :] > 0, scores, -1000000000.0)
    probs = low(jax.nn.softmax(scores, axis=-1))
    attended = jnp.einsum('whqk,wkhd->wqhd', probs, value_heads, precision=highest).reshape(window_count, token_count, feature_count)
    attended = low_back(low(attended))
    branch = low_back(jnp.einsum('wtd,dc->wtc', attended, outward, precision=highest) + out_bias)
    midway = values + branch
    normed_two = low(layer_norm(midway, gain_two, shift_two))
    hidden = low_back(jnp.einsum('wtc,cf->wtf', normed_two, up_proj, precision=highest) + up_offset)
    active = low(jax.nn.gelu(hidden, approximate=False))
    mixed_out = low_back(jnp.einsum('wtf,fc->wtc', active, down_proj, precision=highest) + down_offset)
    return midway + mixed_out

def shift_windows(values, east_next):
    return jnp.concatenate([values[:, HALF:], values[east_next, :HALF]], axis=1)

def unshift_windows(values, east_next):
    west_prev = jnp.argsort(east_next)
    return jnp.concatenate([values[west_prev, HALF:], values[:, :HALF]], axis=1)

def pick_block(params, index):
    return tuple((param[index] for param in params))

def group(windows, valid_tokens, east_next, params):
    first_out = low(block(windows, valid_tokens, pick_block(params, 0)))
    shifted = low_back(shift_windows(first_out, east_next))
    shifted_valid = shift_windows(valid_tokens, east_next)
    second_out = low(block(shifted, shifted_valid, pick_block(params, 1)))
    return unshift_windows(second_out, east_next) * valid_tokens[..., None]

def reference(tokens, token_mask, shift_next, cotangent, attend_gain, attend_shift, inward_weight, inward_bias, earth_bias, outward_weight, outward_bias, mixer_gain, mixer_shift, up_weight, up_bias, down_weight, down_bias):
    windows = tokens.astype(jnp.float32).reshape(N_DP, HOME, WIN, C)
    valid_all = token_mask.astype(jnp.float32).reshape(N_DP, HOME, WIN)
    next_all = shift_next.reshape(N_DP, HOME)
    params = tuple((param.astype(jnp.float32) for param in (attend_gain, attend_shift, inward_weight, inward_bias, earth_bias, outward_weight, outward_bias, mixer_gain, mixer_shift, up_weight, up_bias, down_weight, down_bias)))

    def whole(windows_in, params_in):
        rounded = low_back(windows_in)

        def run(items):
            return group(items[0], items[1], items[2], params_in)
        return lax.map(jax.checkpoint(run), (rounded, valid_all, next_all))
    outputs, backward = jax.vjp(whole, windows, params)
    window_grad, param_grads = backward(cotangent.astype(jnp.float32).reshape(N_DP, HOME, WIN, C))
    block_output = outputs.reshape(PACKS, WIN, C).astype(jnp.bfloat16)
    tokens_grad = window_grad.reshape(PACKS, WIN, C).astype(jnp.bfloat16)
    return (block_output, tokens_grad, param_grads[0], param_grads[1], param_grads[2], param_grads[3], param_grads[4], param_grads[5], param_grads[6], param_grads[7], param_grads[8], param_grads[9], param_grads[10], param_grads[11], param_grads[12])
```

```python
import functools

import jax
import jax.numpy as jnp
from jax import lax
from jax.experimental import pallas as pl
from jax.experimental.pallas import tpu as pltpu
from jax.sharding import PartitionSpec as P

F32 = jnp.float32
BF16 = jnp.bfloat16
I32 = jnp.int32

CHUNK = 8
TILE = 2
LATS = 6
HALF_COLS = 6
NEVER = -1000000000.0
VMEM_LIMIT = 60 * 1024 * 1024


def mm(a, b):
    return lax.dot_general(a, b, (((1,), (0,)), ((), ())), preferred_element_type=F32)


def mm_nt(a, b):
    return lax.dot_general(a, b, (((1,), (1,)), ((), ())), preferred_element_type=F32)


def mm_tn(a, b):
    return lax.dot_general(a, b, (((0,), (0,)), ((), ())), preferred_element_type=F32)


def fold_rows(values):
    rows, width = values.shape
    return jnp.sum(values.reshape(rows // 8, 8, width), axis=0)


def plan_kernel(t_ref, mask_ref, next_ref, meta_ref, tab_ref, place_ref, seen, order, first, last, rows, cols):
    home = next_ref.shape[0]
    cap = tab_ref.shape[1]
    half = mask_ref.shape[1] // 2
    t = t_ref[0]

    def clear(s, carry):
        seen[s] = 0
        place_ref[0, s] = -1
        place_ref[1, s] = -1
        high = mask_ref[s, 0]
        for i in range(1, LATS):
            high += mask_ref[s, i * HALF_COLS]
        wide = mask_ref[s, 0] + mask_ref[s, half]
        for j in range(1, HALF_COLS):
            wide += mask_ref[s, j] + mask_ref[s, half + j]
        rows[s] = high
        cols[s] = wide
        return carry

    lax.fori_loop(0, home, clear, 0)

    def visit(origin, count):
        fresh = (rows[origin] > 0) & (seen[origin] == 0)

        def walk(carry):
            s, at, _ = carry
            seen[s] = 1
            order[at] = s
            first[at] = count
            following = next_ref[s]
            return following, at + 1, (following != origin) & (at + 1 < home)

        return lax.while_loop(lambda carry: carry[2], walk, (origin, count, fresh))[1]

    total = lax.fori_loop(0, home, visit, 0)

    def close(back, carry):
        p = total - 1 - back
        after = jnp.minimum(p + 1, home - 1)
        ends = (p == total - 1) | (first[after] != first[p])
        end = jnp.where(ends, p, carry)
        last[p] = end
        return end

    lax.fori_loop(0, total, close, 0)

    cut = (total + 1) // 2
    base = t * cut
    n = jnp.where(t == 0, cut, total - cut)

    def fill(i, carry):
        live = i < n
        p = jnp.where(live, base + i, 0)
        slot = jnp.where(live, order[p], 0)
        ahead = jnp.where(p == last[p], first[p], p + 1)
        behind = jnp.where(p == first[p], last[p], p - 1)
        next_slot = next_ref[slot]
        ahead_in = live & (ahead >= base) & (ahead < base + n)
        behind_in = live & (behind >= base) & (behind < base + n)
        tab_ref[0, i] = slot
        tab_ref[1, i] = jnp.where(ahead_in, ahead - base, -1)
        tab_ref[2, i] = jnp.where(behind_in, behind - base, -1)
        tab_ref[3, i] = jnp.where(live, rows[slot], 0)
        tab_ref[4, i] = jnp.where(live, cols[slot], 0)
        tab_ref[5, i] = jnp.where(live, rows[next_slot], 0)
        tab_ref[6, i] = jnp.where(live, cols[next_slot], 0)
        tab_ref[7, i] = jnp.where(live, next_slot, 0)
        return carry

    @pl.when(total == 0)
    def _():
        order[0] = 0
        first[0] = 0
        last[0] = 0

    lax.fori_loop(0, cap, fill, 0)

    def settle(p, carry):
        slot = order[p]
        owner = jnp.where(p >= cut, 1, 0)
        here = p - owner * cut
        source = jnp.where(owner == t, here, cap + here)
        place_ref[0, slot] = source
        place_ref[1, jnp.where(t == 1, slot, next_ref[slot])] = source
        return carry

    lax.fori_loop(0, total, settle, 0)

    crossing = (cut < total) & (first[jnp.minimum(cut, home - 1)] < cut)
    tail = jnp.maximum(cut - 1, 0)
    meta_ref[0] = n
    meta_ref[1] = jnp.where(crossing & (t == 0), first[jnp.minimum(cut, home - 1)], 0)
    meta_ref[2] = jnp.where(t == 0, tail, jnp.where(crossing, last[tail] - cut, 0))
    meta_ref[3] = t
    for spare in range(4, 8):
        meta_ref[spare] = 0


def make_plan(part, token_mask, shift_next, cap):
    home = shift_next.shape[0]
    smem = pl.BlockSpec(memory_space=pltpu.SMEM)
    return pl.pallas_call(
        plan_kernel,
        out_shape=(
            jax.ShapeDtypeStruct((8,), I32),
            jax.ShapeDtypeStruct((8, cap), I32),
            jax.ShapeDtypeStruct((2, home), I32),
        ),
        in_specs=[smem, smem, smem],
        out_specs=(smem, smem, smem),
        scratch_shapes=[pltpu.SMEM((home,), I32) for _ in range(6)],
        name="plan",
    )(part, token_mask, shift_next)


def gelu_pair(u):
    a = jnp.abs(u)
    t = pl.reciprocal(1.0 + 0.23164189 * a, approx=True)
    bell = jnp.exp(-0.5 * (u * u))
    poly = t * (
        0.127414796 + t * (-0.142248368 + t * (0.7107068705 + t * (-0.7265760135 + t * 0.5307027145)))
    )
    low = poly * bell
    cdf = jnp.where(u >= 0.0, 1.0 - low, low)
    return u * cdf, cdf + u * (0.3989422804 * bell)


def normalise(values):
    centred = values - jnp.mean(values, axis=-1, keepdims=True)
    spread = jnp.mean(centred * centred, axis=-1, keepdims=True)
    scale = lax.rsqrt(spread + 1e-05)
    return centred * scale, scale


def norm_back(grad, unit, scale, gain):
    inner = grad * gain
    mean_one = jnp.mean(inner, axis=-1, keepdims=True)
    mean_two = jnp.mean(inner * unit, axis=-1, keepdims=True)
    return scale * (inner - mean_one - unit * mean_two)


def block_kernel(shifted, train, index, head_width, *refs):
    refs = list(refs)
    take = lambda count: [refs.pop(0) for _ in range(count)]
    meta, tab, src_own, src_oth = take(4)
    if train:
        up_own, up_oth = take(2)
    (
        lat_lane,
        col_lane,
        lat_row,
        col_row,
        gain_one,
        shift_one,
        out_bias,
        gain_two,
        shift_two,
        down_bias,
    ) = take(10)
    inward, entry, earth, outward, up, up_bias, down = ([r, s] for r, s in zip(take(7), take(7)))
    if train:
        if shifted:
            keep, send = take(2)
        back_one, back_two = take(2)
        g_in, g_earth, g_out, g_up, g_down = ([r, s] for r, s in zip(take(5), take(5)))
        g_small, g_hidden, g_entry = take(3)
    else:
        fwd_out, fwd_half = take(2)
    xs, x_sem, wqkv, wo, bqkv, h1, qkv, att, mid, h2, act = take(11)
    if train:
        rs, r_sem, slope, probs, rr, dmid, da, do, acc_in, acc_earth, acc_out, acc_up, acc_down, acc_small, acc_hidden, acc_entry = take(16)
    assert not refs

    cap = tab.shape[1]
    half = xs.shape[2]
    win = 2 * half
    width = xs.shape[3]
    own_heads = earth[0].shape[0]
    heads = 2 * own_heads
    part = width // 2
    groups = width // 128
    per_group = 128 // head_width
    scale = head_width**-0.5
    hidden_part = up[0].shape[1]
    pieces = [(s, at) for s in range(2) for at in range(0, hidden_part, 384)]
    n = meta[0]
    t = meta[3]
    chunks = (n + CHUNK - 1) // CHUNK
    lanes = lax.broadcasted_iota(I32, (1, 128), 1) // head_width
    head_keep = [jnp.where(lanes == k, 1.0, 0.0).astype(BF16) for k in range(per_group)]

    def by_part(west, one, other, index_, dst, sem):
        is_own = t == (0 if west else 1)

        @pl.when(is_own)
        def _():
            pltpu.make_async_copy(one.at[index_], dst, sem).start()

        @pl.when(jnp.logical_not(is_own))
        def _():
            pltpu.make_async_copy(other.at[index_], dst, sem).start()

    def by_place(local, local_half, one, other, dst, sem):
        @pl.when(local >= 0)
        def _():
            pltpu.make_async_copy(one.at[local, local_half], dst, sem).start()

        @pl.when(local < 0)
        def _():
            pltpu.make_async_copy(other, dst, sem).start()

    def start_loads(i, carry):
        if shifted:
            by_place(i, 1, src_own, src_oth, xs.at[i, 0], x_sem.at[i, 0])
            by_place(tab[1, i], 0, src_own, src_oth, xs.at[i, 1], x_sem.at[i, 1])
        else:
            by_part(True, src_own, src_oth, tab[0, i], xs.at[i, 0], x_sem.at[i, 0])
            by_part(False, src_own, src_oth, tab[0, i], xs.at[i, 1], x_sem.at[i, 1])
        if train:
            if shifted:
                by_part(False, up_own, up_oth, tab[0, i], rs.at[i, 0], r_sem.at[i, 0])
                by_part(True, up_own, up_oth, tab[7, i], rs.at[i, 1], r_sem.at[i, 1])
            else:
                by_place(tab[2, i], 1, up_own, up_oth, rs.at[i, 0], r_sem.at[i, 0])
                by_place(i, 0, up_own, up_oth, rs.at[i, 1], r_sem.at[i, 1])
        return carry

    lax.fori_loop(0, n, start_loads, 0)

    def blank(i, carry):
        for k in range(2):
            xs[i, k] = jnp.zeros_like(xs[i, k])
            if train:
                rs[i, k] = jnp.zeros_like(rs[i, k])
        return carry

    lax.fori_loop(n, chunks * CHUNK, blank, 0)

    for j in range(3):
        for s in range(2):
            wqkv[:, j * width + s * part : j * width + (s + 1) * part] = inward[s][j]
    for s in range(2):
        wo[s * part : (s + 1) * part, :] = outward[s][...]
    bqkv[...] = jnp.zeros_like(bqkv)
    for s in range(2):
        bqkv[0:1, s * part : (s + 1) * part] = entry[s][index, 0:1, :]
        bqkv[0:1, 2 * width + s * part : 2 * width + (s + 1) * part] = entry[s][index, 1:2, :]
    if train:
        for ref in (acc_in, acc_earth, acc_out, acc_up, acc_down, acc_small, acc_hidden, acc_entry):
            ref[...] = jnp.zeros_like(ref)

    def row(ref):
        return ref[index : index + 1, :]

    def extents(i):
        high, wide, high_next, wide_next = tab[3, i], tab[4, i], tab[5, i], tab[6, i]
        if shifted:
            return (high, wide - HALF_COLS), (high_next, wide_next)
        return (high, wide), (high, wide - HALF_COLS)

    def valid_rows(i, k):
        high, wide = extents(i)[k]
        return (lat_row[...] < high) & (col_row[...] < wide)

    def window_x(i):
        return jnp.concatenate([xs[i, 0].astype(F32), xs[i, 1].astype(F32)], axis=0)

    def chunk_body(chunk, carry):
        w0 = chunk * CHUNK

        def wait_loads(i, c):
            for k in range(2):
                pltpu.make_async_copy(xs.at[i, k], xs.at[i, k], x_sem.at[i, k]).wait()
                if train:
                    pltpu.make_async_copy(rs.at[i, k], rs.at[i, k], r_sem.at[i, k]).wait()
            return c

        lax.fori_loop(w0, jnp.minimum(w0 + CHUNK, n), wait_loads, 0)

        def entrance(tile, c):
            at = pl.multiple_of(tile * (TILE * win), TILE * win)
            x = jnp.concatenate([window_x(w0 + tile * TILE + j) for j in range(TILE)], axis=0)
            unit, _ = normalise(x)
            low = (unit * row(gain_one) + row(shift_one)).astype(BF16)
            h1[pl.ds(at, TILE * win), :] = low
            for j in range(3):
                cols = slice(j * width, (j + 1) * width)
                value = mm(low, wqkv[:, cols]) + bqkv[0:1, cols]
                if j == 0:
                    value = value * scale
                qkv[pl.ds(at, TILE * win), cols] = value.astype(BF16)
            return c

        lax.fori_loop(0, CHUNK // TILE, entrance, 0)

        def attend(w, c):
            at = pl.multiple_of(w * win, win)
            (high_a, wide_a), (high_b, wide_b) = extents(w0 + w)
            first = lax.broadcasted_iota(I32, (1, win), 1) < half
            high = jnp.where(first, high_a, high_b)
            wide = jnp.where(first, wide_a, wide_b)
            hide = jnp.where((lat_lane[...] < high) & (col_lane[...] < wide), 0.0, NEVER)
            for g in range(groups):
                span = [slice(j * width + g * 128, j * width + (g + 1) * 128) for j in range(3)]
                q, k, v = (qkv[pl.ds(at, win), cols] for cols in span)
                total = None
                for u in range(per_group):
                    head = g * per_group + u
                    bias = earth[head // own_heads][head % own_heads]
                    s = mm_nt(q * head_keep[u], k) + bias + hide
                    e = jnp.exp(s - jnp.max(s, axis=-1, keepdims=True))
                    p = e * (1.0 / jnp.sum(e, axis=-1, keepdims=True))
                    low = p.astype(BF16)
                    if train:
                        probs[w, head] = low
                    got = mm(low, v * head_keep[u])
                    total = got if total is None else total + got
                att[pl.ds(at, win), g * 128 : (g + 1) * 128] = total.astype(BF16)
            return c

        lax.fori_loop(0, CHUNK, attend, 0)

        def middle(tile, c):
            at = pl.multiple_of(tile * (TILE * win), TILE * win)
            rows = pl.ds(at, TILE * win)
            x = jnp.concatenate([window_x(w0 + tile * TILE + j) for j in range(TILE)], axis=0)
            v2 = x + mm(att[rows, :], wo[...]) + row(out_bias)
            if train:
                mid[rows, :] = v2
            unit, unit_scale = normalise(v2)
            low = (unit * row(gain_two) + row(shift_two)).astype(BF16)
            if train:
                h2[rows, :] = low
            if train:
                r_parts = []
                for j in range(TILE):
                    i = w0 + tile * TILE + j
                    for k in range(2):
                        r = rs[i, k].astype(F32)
                        if shifted:
                            r = jnp.where(valid_rows(i, k), r, 0.0)
                        r_parts.append(r)
                r = jnp.concatenate(r_parts, axis=0)
                r_low = r.astype(BF16)
                rr[rows, :] = r_low
            result = v2 + row(down_bias)
            d_h2 = None
            for s, off in pieces:
                cols = slice(off, off + 384)
                wide = slice(s * hidden_part + off, s * hidden_part + off + 384)
                u = mm(low, up[s][:, cols]) + up_bias[s][index : index + 1, cols]
                g, gp = gelu_pair(u)
                g = g.astype(BF16)
                if train:
                    act[rows, wide] = g
                if not train or shifted:
                    result = result + mm(g, down[s][cols, :])
                if train:
                    du = mm_nt(r_low, down[s][cols, :]) * gp
                    acc_hidden[:, wide] += fold_rows(du)
                    du = du.astype(BF16)
                    slope[rows, wide] = du
                    d = mm_nt(du, up[s][:, cols])
                    d_h2 = d if d_h2 is None else d_h2 + d
            if not train:
                for j in range(TILE):
                    for k in range(2):
                        a = j * win + k * half
                        fwd_out[w0 + tile * TILE + j, k] = result[a : a + half].astype(BF16)
            elif shifted:
                for j in range(TILE):
                    i = w0 + tile * TILE + j
                    for k in range(2):
                        a = j * win + k * half
                        piece = jnp.where(valid_rows(i, k), result[a : a + half], 0.0).astype(BF16)

                        @pl.when(t == 1 - k)
                        def _(piece=piece, i=i):
                            keep[i] = piece

                        @pl.when(t == k)
                        def _(piece=piece, i=i):
                            send[i] = piece

            if train:
                acc_small[5] += fold_rows(r)
                acc_small[4] += fold_rows(d_h2)
                acc_small[3] += fold_rows(d_h2 * unit)
                dv2 = r + norm_back(d_h2, unit, unit_scale, row(gain_two))
                dmid[rows, :] = dv2
                acc_small[2] += fold_rows(dv2)
                da_low = dv2.astype(BF16)
                da[rows, :] = da_low
                do[rows, :] = mm_nt(da_low, wo[...]).astype(BF16)
            return c

        lax.fori_loop(0, CHUNK // TILE, middle, 0)
        if not train:
            return carry

        def attend_back(w, c):
            at = pl.multiple_of(w * win, win)
            rows = pl.ds(at, win)
            for g in range(groups):
                span = [slice(j * width + g * 128, j * width + (g + 1) * 128) for j in range(3)]
                q, k, v = (qkv[rows, cols] for cols in span)
                dog = do[rows, g * 128 : (g + 1) * 128]
                dq = dk = dv = None
                for u in range(per_group):
                    head = g * per_group + u
                    low = probs[w, head]
                    p = low.astype(F32)
                    dom = dog * head_keep[u]
                    dp = mm_nt(dom, v)
                    ds = p * (dp - jnp.sum(dp * p, axis=-1, keepdims=True))
                    acc_earth[head] += ds
                    ds = ds.astype(BF16)
                    parts = (mm(ds, k * head_keep[u]), mm_tn(ds, q * head_keep[u]), mm_tn(low, dom))
                    if dq is None:
                        dq, dk, dv = parts
                    else:
                        dq, dk, dv = dq + parts[0], dk + parts[1], dv + parts[2]
                dq = dq * scale
                for j, value in ((0, dq), (2, dv)):
                    acc_entry[:, span[j]] += fold_rows(value)
                for j, value in enumerate((dq, dk, dv)):
                    qkv[rows, span[j]] = value.astype(BF16)
            return c

        lax.fori_loop(0, CHUNK, attend_back, 0)

        def exit_back(tile, c):
            at = pl.multiple_of(tile * (TILE * win), TILE * win)
            rows = pl.ds(at, TILE * win)
            x = jnp.concatenate([window_x(w0 + tile * TILE + j) for j in range(TILE)], axis=0)
            unit, unit_scale = normalise(x)
            dh = mm_nt(qkv[rows, :], wqkv[...])
            acc_small[1] += fold_rows(dh)
            acc_small[0] += fold_rows(dh * unit)
            dv = dmid[rows, :] + norm_back(dh, unit, unit_scale, row(gain_one))
            for j in range(TILE):
                i = w0 + tile * TILE + j
                for k in range(2):
                    a = j * win + k * half
                    piece = dv[a : a + half].astype(BF16)
                    if shifted:
                        back_one[i, k] = piece
                    else:

                        @pl.when(t == k)
                        def _(piece=piece, i=i):
                            back_one[i] = piece

                        @pl.when(t == 1 - k)
                        def _(piece=piece, i=i):
                            back_two[i] = piece

            return c

        lax.fori_loop(0, CHUNK // TILE, exit_back, 0)

        r_turned = rr[...].T
        h_turned = h2[...].T

        def hidden_grads(j, c):
            cols = pl.ds(pl.multiple_of(j * 256, 256), 256)
            acc_down[:, cols] += mm(r_turned, act[:, cols])
            acc_up[:, cols] += mm(h_turned, slope[:, cols])
            return c

        for j in range(2 * hidden_part // 256):
            hidden_grads(j, 0)
        acc_out[...] += mm(att[...].T, da[...])
        turned = h1[...].T
        for j in range(3):
            cols = slice(j * width, (j + 1) * width)
            acc_in[:, cols] += mm(turned, qkv[:, cols])
        return carry

    lax.fori_loop(0, chunks, chunk_body, 0)

    if not train:
        fwd_half[...] = fwd_out[meta[1], 0]
        return
    if shifted:
        back_two[...] = back_one[meta[2], 1]
    for s in range(2):
        for j in range(3):
            g_in[s][j] = acc_in[:, j * width + s * part : j * width + (s + 1) * part].astype(BF16)
        g_out[s][...] = acc_out[s * part : (s + 1) * part, :].astype(BF16)
        g_up[s][...] = acc_up[:, s * hidden_part : (s + 1) * hidden_part].astype(BF16)
        g_down[s][...] = acc_down[:, s * hidden_part : (s + 1) * hidden_part].astype(BF16)
        for k in range(own_heads):
            g_earth[s][k] = acc_earth[s * own_heads + k].astype(BF16)
    g_small[...] = jnp.sum(acc_small[...], axis=1)
    g_hidden[...] = jnp.sum(acc_hidden[...], axis=0, keepdims=True)
    g_entry[...] = jnp.sum(acc_entry[...], axis=0, keepdims=True)


def run_block(shifted, train, plan, source, upstream, consts, params, mates):
    index = 1 if shifted else 0
    meta, tab, _ = plan
    (gain_one, shift_one, inward, entry, earth, outward, out_bias, gain_two, shift_two, up, up_bias, down, down_bias) = params
    (inward_oth, entry_oth, earth_oth, outward_oth, up_oth, up_bias_oth, down_oth) = mates
    cap = tab.shape[1]
    half, width = source[0].shape[-2:]
    rows = CHUNK * 2 * half
    own_heads = earth.shape[1]
    win = earth.shape[2]
    hidden_part = up.shape[2]
    hidden = 2 * hidden_part
    head_width = width // (2 * own_heads)
    once = pl.Buffered(1)
    smem = pl.BlockSpec(memory_space=pltpu.SMEM)
    hbm = pl.BlockSpec(memory_space=pl.ANY)

    def whole(array):
        zeros = (0,) * array.ndim
        return pl.BlockSpec(array.shape, lambda i: zeros, pipeline_mode=once)

    def of_block(array):
        at = (index,) + (0,) * (array.ndim - 1)
        return pl.BlockSpec((None,) + array.shape[1:], lambda i: at, pipeline_mode=once)

    inputs, specs = [], []

    def add(array, spec):
        inputs.append(array)
        specs.append(spec)

    add(meta, smem)
    add(tab, smem)
    for array in (*source, *(upstream or ())):
        add(array, hbm)
    for array in consts:
        add(array, whole(array))
    for array in (gain_one, shift_one, out_bias, gain_two, shift_two, down_bias):
        add(array, whole(array))
    for group in (
        (inward, entry, earth, outward, up, up_bias, down),
        (inward_oth, entry_oth, earth_oth, outward_oth, up_oth, up_bias_oth, down_oth),
    ):
        for place, array in enumerate(group):
            add(array, whole(array) if place in (1, 5) else of_block(array))

    half_shape = (half, width)
    outs = []
    if not train:
        outs += [((cap, 2) + half_shape, BF16), (half_shape, BF16)]
    else:
        if shifted:
            outs += [((cap,) + half_shape, BF16)] * 2
            outs += [((cap, 2) + half_shape, BF16), (half_shape, BF16)]
        else:
            outs += [((cap,) + half_shape, BF16)] * 2
        for _ in range(2):
            outs += [
                ((3, width, width // 2), BF16),
                ((own_heads, win, win), BF16),
                ((width // 2, width), BF16),
                ((width, hidden_part), BF16),
                ((width, hidden_part), BF16),
            ]
        outs += [((6, width), F32), ((1, hidden), F32), ((1, 3 * width), F32)]
    out_shape = tuple(jax.ShapeDtypeStruct(shape, dtype) for shape, dtype in outs)
    out_specs = tuple(whole(s) for s in out_shape)

    scratch = [
        pltpu.VMEM((cap, 2) + half_shape, BF16),
        pltpu.SemaphoreType.DMA((cap, 2)),
        pltpu.VMEM((width, 3 * width), BF16),
        pltpu.VMEM((width, width), BF16),
        pltpu.VMEM((8, 3 * width), F32),
        pltpu.VMEM((rows, width), BF16),
        pltpu.VMEM((rows, 3 * width), BF16),
        pltpu.VMEM((rows, width), BF16),
        pltpu.VMEM((rows, width) if train else (8, 128), F32),
        pltpu.VMEM((rows, width) if train else (16, 128), BF16),
        pltpu.VMEM((rows, hidden) if train else (16, 128), BF16),
    ]
    if train:
        scratch += [
            pltpu.VMEM((cap, 2) + half_shape, BF16),
            pltpu.SemaphoreType.DMA((cap, 2)),
            pltpu.VMEM((rows, hidden), BF16),
            pltpu.VMEM((CHUNK, 2 * own_heads, win, win), BF16),
            pltpu.VMEM((rows, width), BF16),
            pltpu.VMEM((rows, width), F32),
            pltpu.VMEM((rows, width), BF16),
            pltpu.VMEM((rows, width), BF16),
            pltpu.VMEM((width, 3 * width), F32),
            pltpu.VMEM((2 * own_heads, win, win), F32),
            pltpu.VMEM((width, width), F32),
            pltpu.VMEM((width, hidden), F32),
            pltpu.VMEM((width, hidden), F32),
            pltpu.VMEM((6, 8, width), F32),
            pltpu.VMEM((8, hidden), F32),
            pltpu.VMEM((8, 3 * width), F32),
        ]
    return pl.pallas_call(
        functools.partial(block_kernel, shifted, train, index, head_width),
        grid=(1,),
        out_shape=out_shape,
        in_specs=specs,
        out_specs=out_specs,
        scratch_shapes=scratch,
        compiler_params=pltpu.CompilerParams(vmem_limit_bytes=VMEM_LIMIT),
        name=("second" if shifted else "first") + ("_train" if train else "_ahead"),
    )(*inputs)


def settle_kernel(place, keep_a, recv_a, keep_b, recv_b, out_a, out_b, zeros, sems):
    home = place.shape[1]
    cap = keep_a.shape[0]
    zeros[...] = jnp.zeros_like(zeros)

    def start(s, carry):
        for j, (keep, recv, out) in enumerate(((keep_a, recv_a, out_a), (keep_b, recv_b, out_b))):
            source = place[j, s]

            @pl.when(source < 0)
            def _(out=out, j=j):
                pltpu.make_async_copy(zeros, out.at[s], sems.at[j, s]).start()

            @pl.when((source >= 0) & (source < cap))
            def _(keep=keep, out=out, j=j, source=source):
                pltpu.make_async_copy(keep.at[source], out.at[s], sems.at[j, s]).start()

            @pl.when(source >= cap)
            def _(recv=recv, out=out, j=j, source=source):
                pltpu.make_async_copy(recv.at[source - cap], out.at[s], sems.at[j, s]).start()

        return carry

    lax.fori_loop(0, home, start, 0)

    def finish(s, carry):
        for j, out in enumerate((out_a, out_b)):
            pltpu.make_async_copy(zeros, out.at[s], sems.at[j, s]).wait()
        return carry

    lax.fori_loop(0, home, finish, 0)


def settle(place, pair_a, pair_b):
    home = place.shape[1]
    half_shape = pair_a[0].shape[1:]
    hbm = pl.BlockSpec(memory_space=pl.ANY)
    shape = jax.ShapeDtypeStruct((home,) + half_shape, BF16)
    return pl.pallas_call(
        settle_kernel,
        out_shape=(shape, shape),
        in_specs=[pl.BlockSpec(memory_space=pltpu.SMEM)] + [hbm] * 4,
        out_specs=(hbm, hbm),
        scratch_shapes=[pltpu.VMEM(half_shape, BF16), pltpu.SemaphoreType.DMA((2, home))],
        name="settle",
    )(place, *pair_a, *pair_b)


def across(value):
    return lax.ppermute(value, "tensor", [(0, 1), (1, 0)])


def local(
    tokens,
    token_mask,
    shift_next,
    cotangent,
    attend_gain,
    attend_shift,
    inward_weight,
    inward_bias,
    earth_bias,
    outward_weight,
    outward_bias,
    mixer_gain,
    mixer_shift,
    up_weight,
    up_bias,
    down_weight,
    down_bias,
):
    home, half, width = tokens.shape
    cap = home // 2
    part = lax.axis_index("tensor").astype(I32).reshape(1)
    tokens_oth = across(tokens)
    inward = jnp.transpose(inward_weight, (0, 2, 1, 3))
    sharded = (inward, inward_bias, earth_bias, outward_weight, up_weight, up_bias, down_weight)
    mates = tuple(across(value) for value in sharded)
    cotangent_oth = across(cotangent)
    plan = make_plan(part, token_mask, shift_next, cap)
    params = (
        attend_gain,
        attend_shift,
        inward,
        inward_bias,
        earth_bias,
        outward_weight,
        outward_bias,
        mixer_gain,
        mixer_shift,
        up_weight,
        up_bias,
        down_weight,
        down_bias,
    )
    win = 2 * half
    token = jnp.arange(win, dtype=I32)
    lat = (token % half) % (LATS * HALF_COLS) // HALF_COLS
    col = token % HALF_COLS
    consts = (
        lat.reshape(1, win),
        col.reshape(1, win),
        jnp.broadcast_to(lat[:half, None], (half, width)),
        jnp.broadcast_to(col[:half, None], (half, width)),
    )

    def train(shifted, source, upstream):
        return run_block(shifted, True, plan, source, upstream, consts, params, mates)

    ahead, ahead_half = run_block(False, False, plan, (tokens, tokens_oth), None, consts, params, mates)
    keep_b, send_b, dz, dz_half, *grads_two = train(
        True, (ahead, across(ahead_half)), (cotangent, cotangent_oth)
    )
    recv_b = across(send_b)
    keep_a, send_a, *grads_one = train(False, (tokens, tokens_oth), (dz, across(dz_half)))
    recv_a = across(send_a)
    tokens_grad, block_output = settle(plan[2], (keep_a, recv_a), (keep_b, recv_b))

    own, other = [], []
    for grads in (grads_one, grads_two):
        own.append(grads[:5])
        other.append(grads[5:10])
    own_two = [jnp.stack(pair).astype(F32) for pair in zip(*own)]
    oth_two = [across(jnp.stack(pair)).astype(F32) for pair in zip(*other)]
    sums = [lax.psum((a + b).astype(BF16), "dp").astype(F32) for a, b in zip(own_two, oth_two)]
    g_in, g_earth, g_out, g_up, g_down = sums
    small = jnp.stack([grads_one[10], grads_two[10]])
    hidden = jnp.stack([grads_one[11][0], grads_two[11][0]])
    entry = jnp.stack([grads_one[12][0].reshape(3, width), grads_two[12][0].reshape(3, width)])[:, 0::2]
    hp = up_weight.shape[2]
    hp_in = width // 2
    hidden = hidden[:, :hp] + across(hidden[:, hp:])
    entry = entry[:, :, :hp_in] + across(entry[:, :, hp_in:])
    small = lax.psum(small, ("dp", "tensor"))
    hidden, entry = lax.psum((hidden, entry), "dp")
    return (
        block_output,
        tokens_grad,
        small[:, 0],
        small[:, 1],
        jnp.transpose(g_in, (0, 2, 1, 3)),
        entry,
        g_earth,
        g_out,
        small[:, 2],
        small[:, 3],
        small[:, 4],
        g_up,
        hidden,
        jnp.transpose(g_down, (0, 2, 1)),
        small[:, 5],
    )


def solution(mesh):
    placed = (
        P("dp", "tensor", None),
        P("dp", None),
        P("dp"),
        P("dp", "tensor", None),
        P(),
        P(),
        P(None, None, None, "tensor"),
        P(None, None, "tensor"),
        P(None, "tensor", None, None),
        P(None, "tensor", None),
        P(),
        P(),
        P(),
        P(None, None, "tensor"),
        P(None, "tensor"),
        P(None, "tensor", None),
        P(),
    )
    return jax.shard_map(
        local,
        mesh=mesh,
        in_specs=placed,
        out_specs=(
            P("dp", "tensor", None),
            P("dp", "tensor", None),
            P(),
            P(),
            P(None, None, None, "tensor"),
            P(None, None, "tensor"),
            P(None, "tensor", None, None),
            P(None, "tensor", None),
            P(),
            P(),
            P(),
            P(None, None, "tensor"),
            P(None, "tensor"),
            P(None, "tensor", None),
            P(),
        ),
        check_vma=False,
    )
```

```python
import functools
from types import SimpleNamespace as Bag

import jax
import jax.numpy as jnp
from jax import lax
from jax.experimental import pallas as pl
from jax.experimental.pallas import tpu as pltpu
from jax.sharding import PartitionSpec as P

F32 = jnp.float32
BF16 = jnp.bfloat16
I32 = jnp.int32

CHUNK = 4
TILE = 4
DP = "dp"
TENSOR = "tensor"
LATS = 6
HALF_COLS = 6
COST_CUT = 64
PARTS = 1
LN2 = 0.6931471805599453
NEVER = -1000000000.0
VMEM_LIMIT = 60 * 1024 * 1024


def mm(a, b):
    return lax.dot_general(a, b, (((1,), (0,)), ((), ())), preferred_element_type=F32)


def mm_nt(a, b):
    return lax.dot_general(a, b, (((1,), (1,)), ((), ())), preferred_element_type=F32)


def mm_tn(a, b):
    return lax.dot_general(a, b, (((0,), (0,)), ((), ())), preferred_element_type=F32)


def fold_rows(values):
    rows, width = values.shape
    return jnp.sum(values.reshape(rows // 8, 8, width), axis=0)


def plan_kernel(t_ref, mask_ref, next_ref, meta_ref, tab_ref, place_ref, seen, order, first, last, rows, cols):
    home = next_ref.shape[0]
    cap = tab_ref.shape[1]
    half = mask_ref.shape[1] // 2
    t = t_ref[0]

    def clear(s, carry):
        seen[s] = 0
        place_ref[0, s] = -1
        place_ref[1, s] = -1
        high = mask_ref[s, 0]
        for i in range(1, LATS):
            high += mask_ref[s, i * HALF_COLS]
        wide = mask_ref[s, 0] + mask_ref[s, half]
        for j in range(1, HALF_COLS):
            wide += mask_ref[s, j] + mask_ref[s, half + j]
        rows[s] = high
        cols[s] = wide
        return carry

    lax.fori_loop(0, home, clear, 0)

    def visit(origin, count):
        fresh = (rows[origin] > 0) & (seen[origin] == 0)

        def walk(carry):
            s, at, _ = carry
            seen[s] = 1
            order[at] = s
            first[at] = count
            following = next_ref[s]
            return following, at + 1, (following != origin) & (at + 1 < home)

        return lax.while_loop(lambda carry: carry[2], walk, (origin, count, fresh))[1]

    total = lax.fori_loop(0, home, visit, 0)

    def close(back, carry):
        p = total - 1 - back
        after = jnp.minimum(p + 1, home - 1)
        ends = (p == total - 1) | (first[after] != first[p])
        end = jnp.where(ends, p, carry)
        last[p] = end
        return end

    lax.fori_loop(0, total, close, 0)

    cut = (total + 1) // 2
    base = t * cut
    n = jnp.where(t == 0, cut, total - cut)

    def fill(i, carry):
        live = i < n
        p = jnp.where(live, base + i, 0)
        slot = jnp.where(live, order[p], 0)
        ahead = jnp.where(p == last[p], first[p], p + 1)
        behind = jnp.where(p == first[p], last[p], p - 1)
        next_slot = next_ref[slot]
        ahead_in = live & (ahead >= base) & (ahead < base + n)
        behind_in = live & (behind >= base) & (behind < base + n)
        tab_ref[0, i] = slot
        tab_ref[1, i] = jnp.where(ahead_in, ahead - base, -1)
        tab_ref[2, i] = jnp.where(behind_in, behind - base, -1)
        tab_ref[3, i] = jnp.where(live, rows[slot], 0)
        tab_ref[4, i] = jnp.where(live, cols[slot], 0)
        tab_ref[5, i] = jnp.where(live, rows[next_slot], 0)
        tab_ref[6, i] = jnp.where(live, cols[next_slot], 0)
        tab_ref[7, i] = jnp.where(live, next_slot, 0)
        return carry

    @pl.when(total == 0)
    def _():
        order[0] = 0
        first[0] = 0
        last[0] = 0

    lax.fori_loop(0, cap, fill, 0)

    def settle(p, carry):
        slot = order[p]
        owner = jnp.where(p >= cut, 1, 0)
        here = p - owner * cut
        source = jnp.where(owner == t, here, cap + here)
        place_ref[0, slot] = source
        place_ref[1, jnp.where(t == 1, slot, next_ref[slot])] = source
        return carry

    lax.fori_loop(0, total, settle, 0)

    crossing = (cut < total) & (first[jnp.minimum(cut, home - 1)] < cut)
    tail = jnp.maximum(cut - 1, 0)
    meta_ref[0] = n
    meta_ref[1] = jnp.where(crossing & (t == 0), first[jnp.minimum(cut, home - 1)], 0)
    meta_ref[2] = jnp.where(t == 0, tail, jnp.where(crossing, last[tail] - cut, 0))
    meta_ref[3] = t
    for spare in range(4, 8):
        meta_ref[spare] = 0


def make_plan(part, token_mask, shift_next, cap):
    home = shift_next.shape[0]
    smem = pl.BlockSpec(memory_space=pltpu.SMEM)
    return pl.pallas_call(
        plan_kernel,
        out_shape=(
            jax.ShapeDtypeStruct((8,), I32),
            jax.ShapeDtypeStruct((8, cap), I32),
            jax.ShapeDtypeStruct((2, home), I32),
        ),
        in_specs=[smem, smem, smem],
        out_specs=(smem, smem, smem),
        scratch_shapes=[pltpu.SMEM((home,), I32) for _ in range(6)],
        name="plan",
    )(part, token_mask, shift_next)


def gelu_pair(u):
    cdf = 0.5 + 0.5 * lax.erf(u * 0.7071067811865476)
    return u * cdf, cdf + u * (0.3989422804014327 * jnp.exp(-0.5 * (u * u)))


def normalise(values):
    centred = values - jnp.mean(values, axis=-1, keepdims=True)
    spread = jnp.mean(centred * centred, axis=-1, keepdims=True)
    scale = lax.rsqrt(spread + 1e-05)
    return centred * scale, scale


def norm_back(grad, unit, scale, gain):
    inner = grad * gain
    mean_one = jnp.mean(inner, axis=-1, keepdims=True)
    mean_two = jnp.mean(inner * unit, axis=-1, keepdims=True)
    return scale * (inner - mean_one - unit * mean_two)


def block_kernel(names, stages, index, head_width, span_of, *refs):
    ref = Bag(**dict(zip(names, refs, strict=True)))
    ahead, mixer, attention = stages
    if ahead or attention:
        in_sides = (ref.in_own, ref.in_oth)
    if ahead or mixer:
        out_sides, up_sides, down_sides = ((ref.out_own, ref.out_oth), (ref.up_own, ref.up_oth), (ref.down_own, ref.down_oth))
    if ahead:
        earth_sides, entry_sides = (ref.earth_own, ref.earth_oth), (ref.entry_own, ref.entry_oth)
        up_bias_sides = (ref.up_bias_own, ref.up_bias_oth)
    if mixer or attention:
        pack_sides = (ref.pack_own, ref.pack_oth)
    shifted = index == 1
    meta, tab = ref.meta, ref.tab
    cap = tab.shape[1]
    half, width = ref.xs.shape[2:]
    win = 2 * half
    rows_all = CHUNK * win
    part = width // 2
    groups = width // 128
    per_group = 128 // head_width
    heads = width // head_width
    own_heads = heads // 2
    scale = head_width**-0.5
    n = meta[0]
    t = meta[3]
    lead, span_count = span_of
    step = pl.program_id(0)
    w0 = lead + step * CHUNK
    first_step = step == 0
    lanes = lax.broadcasted_iota(I32, (1, 128), 1) // head_width
    head_keep = [jnp.where(lanes == k, 1.0, 0.0).astype(BF16) for k in range(per_group)]
    lane = lax.broadcasted_iota(I32, (win, 128), 1)
    spots = [((u + 1) % per_group) * head_width for u in range(per_group)]
    spare_lane = [lane == spot for spot in spots]
    spare_two = [(lane == spot) | (lane == spot + 1) for spot in spots]
    one = jnp.ones((), BF16)
    wide_step = TILE * win

    def row(table):
        return table[index : index + 1, :]

    def by_part(west, one_ref, other, at, dst, sem):
        is_own = t == (0 if west else 1)

        @pl.when(is_own)
        def _():
            pltpu.make_async_copy(one_ref.at[at], dst, sem).start()

        @pl.when(jnp.logical_not(is_own))
        def _():
            pltpu.make_async_copy(other.at[at], dst, sem).start()

    def by_place(local, local_half, one_ref, other, dst, sem):
        @pl.when(local >= 0)
        def _():
            pltpu.make_async_copy(one_ref.at[local, local_half], dst, sem).start()

        @pl.when(local < 0)
        def _():
            pltpu.make_async_copy(other, dst, sem).start()

    xs, x_sem = ref.xs, ref.x_sem
    if mixer:
        rs, r_sem = ref.rs, ref.r_sem

    if ahead:
        bias_copies = [
            pltpu.make_async_copy(
                side.at[index], ref.bias.at[pl.ds(s * own_heads, own_heads)], ref.b_sem.at[s]
            )
            for s, side in enumerate(earth_sides)
        ]

    @pl.when(first_step)
    def _():
        if ahead:
            for copy in bias_copies:
                copy.start()

        def start_loads(i, carry):
            if shifted:
                by_place(i, 1, ref.src, ref.src_oth, xs.at[i, 0], x_sem.at[i, 0])
                by_place(tab[1, i], 0, ref.src, ref.src_oth, xs.at[i, 1], x_sem.at[i, 1])
            else:
                by_part(True, ref.src, ref.src_oth, tab[0, i], xs.at[i, 0], x_sem.at[i, 0])
                by_part(False, ref.src, ref.src_oth, tab[0, i], xs.at[i, 1], x_sem.at[i, 1])
            if mixer and shifted:
                by_part(False, ref.grad_src, ref.grad_oth, tab[0, i], rs.at[i, 0], r_sem.at[i, 0])
                by_part(True, ref.grad_src, ref.grad_oth, tab[7, i], rs.at[i, 1], r_sem.at[i, 1])
            elif mixer:
                by_place(tab[2, i], 1, ref.grad_src, ref.grad_oth, rs.at[i, 0], r_sem.at[i, 0])
                by_place(i, 0, ref.grad_src, ref.grad_oth, rs.at[i, 1], r_sem.at[i, 1])
            return carry

        lax.fori_loop(lead, jnp.minimum(lead + span_count, n), start_loads, 0)

        def blank(i, carry):
            for k in range(2):
                xs[i, k] = jnp.zeros_like(xs[i, k])
                if mixer:
                    rs[i, k] = jnp.zeros_like(rs[i, k])
            return carry

        lax.fori_loop(jnp.maximum(n, lead), lead + span_count, blank, 0)
        if mixer:
            from_head = lax.broadcasted_iota(I32, (width, width), 0) // head_width
            to_head = lax.broadcasted_iota(I32, (width, width), 1) // head_width
            same = from_head // per_group == to_head // per_group
            following = (from_head + 1) % per_group == to_head % per_group
            ref.spread[...] = jnp.where(same & following, 1.0, 0.0).astype(BF16)
        if ahead or attention:
            for j in range(3):
                for s, side in enumerate(in_sides):
                    at = j * width + s * part
                    ref.w_in[at : at + part, :] = side[j]
        if ahead or mixer:
            for s, side in enumerate(out_sides):
                ref.wo[s * part : (s + 1) * part, :] = side[...]
            level = LATS * HALF_COLS
            place = lax.broadcasted_iota(I32, (win, 128), 0)
            inside = place
            for bound in (level, 2 * level, 3 * level):
                inside = inside - jnp.where(place >= bound, level, 0)
            lat = jnp.zeros_like(inside)
            for bound in range(HALF_COLS, level, HALF_COLS):
                lat = lat + jnp.where(inside >= bound, 1, 0)
            ref.lat[...] = lat
            ref.col[...] = inside - HALF_COLS * lat
        if ahead:
            for copy in bias_copies:
                copy.wait()
            for k in range(heads):
                ref.bias[k] = ref.bias[k] * (1.0 / LN2)
        sums = [ref.acc_small] if mixer or attention else []
        if mixer:
            sums += [ref.acc_up, ref.acc_down, ref.acc_hidden]
        if attention:
            sums += [ref.acc_in, ref.acc_out, ref.acc_earth, ref.acc_entry]
        for table in sums:
            table[...] = jnp.zeros_like(table)

    def extents(i):
        high, wide, high_next, wide_next = tab[3, i], tab[4, i], tab[5, i], tab[6, i]
        if shifted:
            return (high, wide - HALF_COLS), (high_next, wide_next)
        return (high, wide), (high, wide - HALF_COLS)

    def valid_rows(i, k):
        high, wide = extents(i)[k]
        valid = (ref.lat[:half] < high) & (ref.col[:half] < wide)
        return jnp.concatenate([jnp.where(valid, 1.0, 0.0)] * groups, axis=1)

    def tile_x(tile):
        parts = []
        for j in range(TILE):
            for k in range(2):
                parts.append(xs[w0 + tile * TILE + j, k].astype(F32))
        return jnp.concatenate(parts, axis=0)

    def entrance(tile, c):
        rows = pl.ds(pl.multiple_of(tile * wide_step, wide_step), wide_step)
        unit, _ = normalise(tile_x(tile))
        low = (unit * row(ref.gain_one) + row(ref.shift_one)).astype(BF16)
        ref.h1[rows, :] = low
        for j in range(3):
            cols = slice(j * width, (j + 1) * width)
            value = mm_nt(low, ref.w_in[cols, :])
            if j != 1:
                value = value + jnp.concatenate(
                    [side[index, j // 2 : j // 2 + 1, :] for side in entry_sides], axis=1
                )
            if j == 0:
                value = value * (scale / LN2)
            ref.qkv[rows, cols] = value.astype(BF16)
        return c

    def attend(pair, c):
        for j in range(2):
            attend_one(pair * 2 + j)
        return c

    def attend_one(w):
        rows = pl.ds(pl.multiple_of(w * win, win), win)
        (high_a, wide_a), (high_b, wide_b) = extents(w0 + w)
        west = lax.broadcasted_iota(I32, (win, 128), 0) < half
        high = jnp.where(west, high_a, high_b)
        wide = jnp.where(west, wide_a, wide_b)
        hide = jnp.where((ref.lat[...] < high) & (ref.col[...] < wide), 0.0, NEVER).astype(BF16)
        for g in range(groups):
            span = [slice(j * width + g * 128, j * width + (g + 1) * 128) for j in range(3)]
            q, k, v = (ref.qkv[rows, cols] for cols in span)
            total = None
            for u in range(per_group):
                head = g * per_group + u
                spare = spare_lane[u]
                s = mm_nt(jnp.where(spare, one, q * head_keep[u]), jnp.where(spare, hide, k))
                s = s + ref.bias[head]
                low = jnp.exp2(s - jnp.max(s, axis=-1, keepdims=True)).astype(BF16)
                ref.probs[w, head] = low
                keep = jnp.broadcast_to(head_keep[u], (win, 128))
                got = mm(low, jnp.concatenate([v * keep, keep], axis=1))
                total = got if total is None else total + got
            inverse = 1.0 / total[:, 128:]
            cols = slice(g * 128, (g + 1) * 128)
            ref.att[rows, cols] = (total[:, :128] * inverse).astype(BF16)
            ref.inverse[rows, cols] = inverse.astype(BF16)

    hidden_part = up_sides[0].shape[1] if ahead or mixer else 0
    hidden = 2 * hidden_part
    pieces = [(s, at) for s in range(2) for at in range(0, hidden_part, 384)]

    def middle(tile, c):
        rows = pl.ds(pl.multiple_of(tile * wide_step, wide_step), wide_step)
        att = ref.att[rows, :]
        v2 = tile_x(tile) + mm(att, ref.wo[...]) + row(ref.out_bias)
        unit, unit_scale = normalise(v2)
        if ahead:
            low = (unit * row(ref.gain_two) + row(ref.shift_two)).astype(BF16)
            ref.h2[rows, :] = low
            result = v2 + row(ref.down_bias)
        if mixer:
            parts = []
            for j in range(TILE):
                i = w0 + tile * TILE + j
                for k in range(2):
                    r = rs[i, k].astype(F32)
                    if shifted:
                        r = r * valid_rows(i, k)
                    parts.append(r)
            r = jnp.concatenate(parts, axis=0)
            r_low = r.astype(BF16)
            ref.rr[rows, :] = r_low
        d_h2 = None
        for s, off in pieces:
            cols = slice(off, off + 384)
            at = off + s * hidden_part
            span = slice(at, at + 384)
            if ahead:
                u = mm(low, up_sides[s][:, cols]) + up_bias_sides[s][index : index + 1, cols]
                g, slope = gelu_pair(u)
                g = g.astype(BF16)
                ref.act[rows, span] = g
                result = result + mm(g, down_sides[s][cols, :])
                if not mixer:
                    ref.slope[rows, span] = slope.astype(BF16)
            else:
                slope = ref.slope[rows, span].astype(F32)
            if mixer:
                du = mm_nt(r_low, down_sides[s][cols, :]) * slope
                ref.acc_hidden[:, span] += fold_rows(du)
                du = du.astype(BF16)
                ref.du[rows, span] = du
                d = mm_nt(du, up_sides[s][:, cols])
                d_h2 = d if d_h2 is None else d_h2 + d
        if ahead:
            for j in range(TILE):
                i = w0 + tile * TILE + j
                for k in range(2):
                    at = j * win + k * half
                    piece = result[at : at + half]
                    if not shifted:
                        ref.out[i, k] = piece.astype(BF16)
                        continue
                    piece = (piece * valid_rows(i, k)).astype(BF16)
                    place_half(ref.keep, ref.send, i, 1 - k, piece)
        if mixer:
            ref.acc_small[5] += fold_rows(r)
            ref.acc_small[4] += fold_rows(d_h2)
            ref.acc_small[3] += fold_rows(d_h2 * unit)
            dv2 = r + norm_back(d_h2, unit, unit_scale, row(ref.gain_two))
            ref.acc_small[2] += fold_rows(dv2)
            da = dv2.astype(BF16)
            ref.da[rows, :] = da
            d_att = mm_nt(da, ref.wo[...]) * ref.inverse[rows, :].astype(F32)
            ref.do[rows, :] = d_att.astype(BF16)
            inner = (d_att * att.astype(F32)).astype(BF16)
            delta = -mm(inner, ref.spread[...])
            high = delta.astype(BF16)
            rest = (delta - high.astype(F32)).astype(BF16)
            spot = lax.broadcasted_iota(I32, (1, width), 1) % head_width
            ref.aug[rows, :] = jnp.where(spot == 0, high, jnp.where(spot == 1, rest, jnp.zeros_like(rest)))
        return c

    def place_half(keep, send, i, owner, piece):
        @pl.when(t == owner)
        def _():
            keep[i] = piece

        @pl.when(t != owner)
        def _():
            send[i] = piece

    def hidden_grads(_, c):
        r_turned = ref.rr[...].T
        h_turned = ref.h2[...].T
        for at in range(0, hidden, 256):
            cols = slice(at, at + 256)
            ref.acc_down[:, cols] += mm(r_turned, ref.act[:, cols])
            ref.acc_up[:, cols] += mm(h_turned, ref.du[:, cols])
        return c

    def attend_back(pair, c):
        spans = [pl.ds(pl.multiple_of((pair * 2 + j) * win, win), win) for j in range(2)]
        for g in range(groups):
            span = [slice(j * width + g * 128, j * width + (g + 1) * 128) for j in range(3)]
            here = slice(g * 128, (g + 1) * 128)
            loaded = []
            for rows in spans:
                q, k, v = (ref.qkv[rows, cols] for cols in span)
                dog = ref.do[rows, here]
                loaded.append((q.T, k, v, dog, dog.T, ref.aug[rows, here], [], [], []))
            for u in range(per_group):
                head = g * per_group + u
                cut = slice(u * head_width, (u + 1) * head_width)
                total = None
                for j in range(2):
                    q_turned, k, v, dog, do_turned, augment, dq, dk, dv = loaded[j]
                    low = ref.probs[pair * 2 + j, head]
                    dom = jnp.where(spare_two[u], augment, dog * head_keep[u])
                    dp = mm_nt(dom, jnp.where(spare_two[u], one, v))
                    ds = low.astype(F32) * dp
                    total = ds if total is None else total + ds
                    ds = ds.astype(BF16)
                    dk.append(mm(q_turned[cut], ds))
                    dv.append(mm(do_turned[cut], low))
                    got = mm(ds, k * head_keep[u])
                    dq[:] = [got if not dq else dq[0] + got]
                ref.acc_earth[head] += total
            for j, rows in enumerate(spans):
                dq, dk, dv = loaded[j][6:]
                dq = dq[0] * scale
                dk = (jnp.concatenate(dk, axis=0) * LN2).T
                dv = jnp.concatenate(dv, axis=0).T
                for at, value in ((0, dq), (2, dv)):
                    ref.acc_entry[:, span[at]] += fold_rows(value)
                for at, value in enumerate((dq, dk, dv)):
                    ref.dqkv[rows, span[at]] = value.astype(BF16)
        return c

    def exit_back(tile, c):
        rows = pl.ds(pl.multiple_of(tile * wide_step, wide_step), wide_step)
        unit, unit_scale = normalise(tile_x(tile))
        dh = mm(ref.dqkv[rows, :], ref.w_in[...])
        ref.acc_small[1] += fold_rows(dh)
        ref.acc_small[0] += fold_rows(dh * unit)
        dv = ref.da[rows, :].astype(F32) + norm_back(dh, unit, unit_scale, row(ref.gain_one))
        for j in range(TILE):
            i = w0 + tile * TILE + j
            for k in range(2):
                at = j * win + k * half
                piece = dv[at : at + half].astype(BF16)
                if shifted:
                    ref.out[i, k] = piece
                else:
                    place_half(ref.keep, ref.send, i - lead, k, piece)
        return c

    def weight_grads(_, c):
        ref.acc_out[...] += mm(ref.att[...].T, ref.da[...])
        turned = ref.h1[...].T
        for j in range(3):
            cols = slice(j * width, (j + 1) * width)
            ref.acc_in[:, cols] += mm(turned, ref.dqkv[:, cols])
        return c

    @pl.when(w0 < n)
    def _():
        def wait_loads(i, c):
            for k in range(2):
                pltpu.make_async_copy(xs.at[i, k], xs.at[i, k], x_sem.at[i, k]).wait()
                if mixer:
                    pltpu.make_async_copy(rs.at[i, k], rs.at[i, k], r_sem.at[i, k]).wait()
            return c

        lax.fori_loop(w0, jnp.minimum(w0 + CHUNK, n), wait_loads, 0)
        if ahead:
            lax.fori_loop(0, CHUNK // TILE, entrance, 0)
            lax.fori_loop(0, CHUNK // 2, attend, 0)
        if ahead or mixer:
            lax.fori_loop(0, CHUNK // TILE, middle, 0)
        if mixer:
            lax.fori_loop(0, 1, hidden_grads, 0)
        if attention:
            lax.fori_loop(0, CHUNK // 2, attend_back, 0)
            lax.fori_loop(0, CHUNK // TILE, exit_back, 0)
            lax.fori_loop(0, 1, weight_grads, 0)

    @pl.when(step == pl.num_programs(0) - 1)
    def _():
        if ahead and not shifted:
            ref.out_half[...] = ref.out[meta[1], 0]
        if attention and shifted:
            ref.out_half[...] = ref.out[meta[2], 1]
        if mixer:
            for s, pack in enumerate(pack_sides):
                base = s * hidden_part
                for at in range(0, hidden_part, width):
                    cols = slice(base + at, base + at + width)
                    pack[at : at + width, :] = ref.acc_up[:, cols].astype(BF16)
                    pack[hidden_part + at : hidden_part + at + width, :] = ref.acc_down[:, cols].astype(BF16)
                if pack.shape[0] > 2 * hidden_part:
                    pack[2 * hidden_part :, :] = jnp.zeros_like(pack[2 * hidden_part :, :])
            ref.sums_small[...] = jnp.sum(ref.acc_small[...], axis=1)
            ref.sums_hidden[...] = jnp.sum(ref.acc_hidden[...], axis=0, keepdims=True)
        if attention:
            small = jnp.sum(ref.acc_small[...], axis=1)
            hidden_sum = ref.sums_hidden[...]
            if lead == 0:
                small = small + ref.sums_small[...]
            else:
                hidden_sum = jnp.zeros_like(hidden_sum)
            half_hidden = hidden_sum.shape[1] // 2
            entry_sum = jnp.sum(ref.acc_entry[...], axis=0, keepdims=True)
            layout = pack_rows(width, own_heads, win)
            for s, pack in enumerate(pack_sides):
                cuts = [slice(j * width + s * part, j * width + (s + 1) * part) for j in range(3)]
                for j, cut in enumerate(cuts):
                    at = layout.inward + j * part
                    pack[at : at + part, :] = ref.acc_in[:, cut].T.astype(BF16)
                pack[layout.out : layout.out + part, :] = ref.acc_out[s * part : (s + 1) * part, :].astype(BF16)
                earth = [ref.acc_earth[s * own_heads + k] for k in range(own_heads)]
                for k, value in enumerate(earth):
                    row_at = layout.earth + (k // 3) * win
                    pack[row_at : row_at + win, (k % 3) * 128 : (k % 3 + 1) * 128] = value[:, :128].astype(BF16)
                rest = jnp.concatenate([value[:, 128:] for value in earth], axis=1)
                rest = jnp.concatenate([rest, jnp.zeros((win, 128 - rest.shape[1]), F32)], axis=1)
                third = win // 3
                for k in range(3):
                    pack[layout.rest : layout.rest + third, k * 128 : (k + 1) * 128] = rest[
                        k * third : (k + 1) * third
                    ].astype(BF16)
                lines = [small]
                for at in range(s * half_hidden, (s + 1) * half_hidden, width):
                    lines.append(hidden_sum[:, at : at + width])
                lines.append(jnp.concatenate([entry_sum[:, cuts[0]], entry_sum[:, cuts[2]]], axis=1))
                count = small.shape[0] + len(lines) - 1
                lines.append(jnp.zeros((16 - count, width), F32))
                pack[layout.small : layout.small + 16, :] = jnp.concatenate(lines, axis=0).astype(BF16)
                if pack.shape[0] > layout.total:
                    pack[layout.total :, :] = jnp.zeros_like(pack[layout.total :, :])


def pack_rows(width, own_heads, win):
    counts = dict(
        inward=3 * width // 2, out=width // 2, earth=own_heads // 3 * win, rest=win // 3, small=16, total=0
    )
    layout, at = {}, 0
    for name, count in counts.items():
        layout[name] = at
        at += count
    return Bag(**layout)


def padded(rows, devices):
    unit = 16 * devices
    return -(-rows // unit) * unit


def run_block(stages, index, given, sizes, devices, split):
    cap, half, width, own_heads, hidden_part = sizes
    ahead, mixer, attention = stages
    shifted = index == 1
    win = 2 * half
    rows = CHUNK * win
    heads = 2 * own_heads
    hidden = 2 * hidden_part
    head_width = width // heads
    which, parts = split
    steps = cap // CHUNK // parts
    lead = which * steps * CHUNK
    smem = pl.BlockSpec(memory_space=pltpu.SMEM)
    hbm = pl.BlockSpec(memory_space=pl.ANY)
    ins, outs, scratch = {}, {}, {}

    def whole(shape):
        zeros = (0,) * len(shape)
        return pl.BlockSpec(shape, lambda c: zeros, pipeline_mode=pl.Buffered(1))

    def take(spec, **arrays):
        for name, array in arrays.items():
            ins[name] = (array, whole(array.shape) if spec is None else spec)

    def take_block(**arrays):
        for name, array in arrays.items():
            at = (index,) + (0,) * (array.ndim - 1)
            spec = pl.BlockSpec((None,) + array.shape[1:], lambda c, at=at: at, pipeline_mode=pl.Buffered(1))
            ins[name] = (array, spec)

    def chunked(shape):
        zeros = (0,) * (len(shape) - 1)
        return pl.BlockSpec(shape, lambda c: (which * steps + c,) + zeros)

    def give(dtype=BF16, **shapes):
        for name, shape in shapes.items():
            outs[name] = (jax.ShapeDtypeStruct(shape, dtype), whole(shape))

    flat = lambda factor: (rows, factor * width)
    stash = dict(
        qkv=flat(3),
        probs=(CHUNK, heads, win, win),
        att=flat(1),
        inverse=flat(1),
        h1=flat(1),
        h2=flat(1),
        act=(rows, hidden),
        slope=(rows, hidden),
        da=flat(1),
        do=flat(1),
        aug=flat(1),
    )

    def carry_in(**arrays):
        for name, array in arrays.items():
            ins[name] = (array, chunked(stash[name]))

    def carry_out(**wanted):
        for name in wanted:
            shape = stash[name]
            full = jax.ShapeDtypeStruct((shape[0] * cap // CHUNK,) + shape[1:], BF16)
            outs[name] = (full, chunked(shape))

    g = given
    take(smem, meta=g.meta, tab=g.tab)
    take(hbm, src=g.src, src_oth=g.src_oth)
    if mixer:
        take(hbm, grad_src=g.grad_src, grad_oth=g.grad_oth)
    if ahead:
        take(hbm, earth_own=g.earth_own, earth_oth=g.earth_oth)
        take(None, shift_one=g.shift_one, shift_two=g.shift_two, down_bias=g.down_bias)
        take(None, entry_own=g.entry_own, entry_oth=g.entry_oth)
        take(None, up_bias_own=g.up_bias_own, up_bias_oth=g.up_bias_oth)
    if ahead or mixer:
        take(None, out_bias=g.out_bias, gain_two=g.gain_two)
        take_block(out_own=g.out_own, out_oth=g.out_oth, up_own=g.up_own, up_oth=g.up_oth)
        take_block(down_own=g.down_own, down_oth=g.down_oth)
    if ahead or attention:
        take(None, gain_one=g.gain_one)
        take_block(in_own=g.in_own, in_oth=g.in_oth)
    if attention:
        take(None, sums_small=g.sums_small, sums_hidden=g.sums_hidden)
        carry_in(qkv=g.qkv, probs=g.probs, att=g.att, h1=g.h1, da=g.da, do=g.do, aug=g.aug)
    elif not ahead:
        carry_in(att=g.att, inverse=g.inverse, h2=g.h2, act=g.act, slope=g.slope)

    half_shape = (half, width)
    if ahead:
        carry_out(qkv=1, probs=1, att=1, h1=1)
        if not mixer:
            carry_out(inverse=1, h2=1, act=1, slope=1)
    if mixer:
        carry_out(da=1, do=1, aug=1)
    if (ahead and not shifted) or (attention and shifted):
        give(out=(cap, 2) + half_shape, out_half=half_shape)
    if (ahead and shifted) or (attention and not shifted):
        give(keep=(cap // parts,) + half_shape, send=(cap // parts,) + half_shape)
    if mixer:
        pack = (padded(2 * hidden_part, devices), width)
        give(pack_own=pack, pack_oth=pack)
        give(F32, sums_small=(6, width), sums_hidden=(1, hidden))
    if attention:
        pack = (padded(pack_rows(width, own_heads, win).total, devices), width)
        give(pack_own=pack, pack_oth=pack)

    def hold(dtype=BF16, **shapes):
        for name, shape in shapes.items():
            scratch[name] = pltpu.VMEM(shape, dtype)

    halves = (cap, 2) + half_shape
    hold(xs=halves)
    scratch.update(x_sem=pltpu.SemaphoreType.DMA((cap, 2)))
    if ahead:
        hold(F32, bias=(heads, win, win))
        scratch.update(b_sem=pltpu.SemaphoreType.DMA((2,)))
    if ahead or attention:
        hold(w_in=(3 * width, width))
    if ahead or mixer:
        hold(wo=(width, width))
        hold(I32, lat=(win, 128), col=(win, 128))
    if ahead and mixer:
        hold(inverse=flat(1), h2=flat(1), act=(rows, hidden))
    if mixer:
        hold(rs=halves, rr=flat(1), du=(rows, hidden), spread=(width, width))
        scratch.update(r_sem=pltpu.SemaphoreType.DMA((cap, 2)))
        hold(F32, acc_up=(width, hidden), acc_down=(width, hidden), acc_hidden=(8, hidden))
    if attention:
        hold(dqkv=flat(3))
        hold(F32, acc_in=(width, 3 * width), acc_out=(width, width))
        hold(F32, acc_earth=(heads, win, win), acc_entry=(8, 3 * width))
    if mixer or attention:
        hold(F32, acc_small=(6, 8, width))

    matmuls = cap * win * (4 * width * width + 2 * width * hidden)
    result = pl.pallas_call(
        functools.partial(
            block_kernel, [*ins, *outs, *scratch], stages, index, head_width, (lead, steps * CHUNK)
        ),
        grid=(steps,),
        out_shape=tuple(shape for shape, _ in outs.values()),
        in_specs=[spec for _, spec in ins.values()],
        out_specs=tuple(spec for _, spec in outs.values()),
        scratch_shapes=list(scratch.values()),
        compiler_params=pltpu.CompilerParams(vmem_limit_bytes=VMEM_LIMIT),
        cost_estimate=pl.CostEstimate(
            flops=2 * sum(stages) * matmuls // COST_CUT,
            bytes_accessed=8 * sum(stages) * cap * win * width * 2 // COST_CUT,
            transcendentals=cap * win * hidden // COST_CUT,
        ),
        name=("ahead" if ahead else "") + ("mixer" if mixer else "") + ("attention" if attention else "") + str(index + 1),
    )(*(array for array, _ in ins.values()))
    return Bag(**dict(zip(outs, result, strict=True)))


def settle_kernel(counts, place, *refs):
    refs = list(refs)
    held = [[refs.pop(0) for _ in range(count)] for count in counts]
    out_a, out_b, zeros, sems = refs
    home = place.shape[1]
    zeros[...] = jnp.zeros_like(zeros)

    def start(s, carry):
        for j, out in enumerate((out_a, out_b)):
            source = place[j, s]

            @pl.when(source < 0)
            def _(out=out, j=j):
                pltpu.make_async_copy(zeros, out.at[s], sems.at[j, s]).start()

            low = 0
            for ref in held[j]:
                high = low + ref.shape[0]

                @pl.when((source >= low) & (source < high))
                def _(ref=ref, out=out, j=j, at=source - low):
                    pltpu.make_async_copy(ref.at[at], out.at[s], sems.at[j, s]).start()

                low = high

        return carry

    lax.fori_loop(0, home, start, 0)

    def finish(s, carry):
        for j, out in enumerate((out_a, out_b)):
            pltpu.make_async_copy(zeros, out.at[s], sems.at[j, s]).wait()
        return carry

    lax.fori_loop(0, home, finish, 0)


def settle(place, first, second):
    home = place.shape[1]
    half_shape = first[0].shape[1:]
    hbm = pl.BlockSpec(memory_space=pl.ANY)
    vmem = pl.BlockSpec(memory_space=pltpu.VMEM)
    shape = jax.ShapeDtypeStruct((home,) + half_shape, BF16)
    counts = (len(first), len(second))
    return pl.pallas_call(
        functools.partial(settle_kernel, counts),
        out_shape=(shape, shape),
        in_specs=[pl.BlockSpec(memory_space=pltpu.SMEM)] + [vmem] * sum(counts),
        out_specs=(hbm, hbm),
        scratch_shapes=[pltpu.VMEM(half_shape, BF16), pltpu.SemaphoreType.DMA((2, home))],
        compiler_params=pltpu.CompilerParams(vmem_limit_bytes=VMEM_LIMIT),
        name="settle",
    )(place, *first, *second)


def local_kernel(jobs, digits_ref, *refs):
    refs = list(refs)
    ins = [[refs.pop(0) for _ in range(count)] for _, count, _, _ in jobs]
    outs = [[refs.pop(0) for _ in range(size if scatter else 1)] for scatter, _, size, _ in jobs]
    assert not refs
    for (scatter, _, size, stage), parts, made in zip(jobs, ins, outs):
        digit = digits_ref[stage]
        if scatter:
            rows = made[0].shape[0]
            for k, out in enumerate(made):
                at = pl.multiple_of((digit ^ k) * rows, rows) if size > 1 else 0
                total = parts[0][pl.ds(at, rows), :].astype(F32)
                for part in parts[1:]:
                    total = total + part[pl.ds(at, rows), :].astype(F32)
                out[...] = total.astype(BF16)
        else:
            rows = parts[0].shape[0]
            for k, part in enumerate(parts):
                made[0][pl.ds(pl.multiple_of((digit ^ k) * rows, rows), rows), :] = part[...]


def dp_groups(devices):
    sizes = []
    while devices > 1:
        size = 4 if devices % 4 == 0 else 2
        sizes.append(size)
        devices //= size
    return sizes


def with_peer(value, stride, k):
    devices = lax.axis_size(DP)
    return lax.ppermute(value, DP, [(d, d ^ (k * stride)) for d in range(devices)])


def stack_kernel(*refs):
    out, pairs = refs[-1], refs[:-1]
    at = 0
    for one, other in zip(pairs[0::2], pairs[1::2]):
        rows = one.shape[0]
        out[at : at + rows, :] = (one[...].astype(F32) + other[...].astype(F32)).astype(BF16)
        at += rows


def stack(*pairs):
    vmem = pl.BlockSpec(memory_space=pltpu.VMEM)
    rows = sum(pair[0].shape[0] for pair in pairs)
    return pl.pallas_call(
        stack_kernel,
        out_shape=jax.ShapeDtypeStruct((rows, pairs[0][0].shape[1]), BF16),
        in_specs=[vmem] * (2 * len(pairs)),
        out_specs=vmem,
        compiler_params=pltpu.CompilerParams(vmem_limit_bytes=VMEM_LIMIT),
        name="stack",
    )(*(value for pair in pairs for value in pair))


class DpSum:
    def __init__(self, parts):
        self.parts = parts
        self.phase = 0
        self.stages, stride = [], 1
        for size in dp_groups(lax.axis_size(DP)):
            self.stages.append((size, stride))
            stride *= size

    def job(self):
        count = len(self.stages)
        if self.phase < count:
            return (True, len(self.parts), self.stages[self.phase][0], self.phase)
        if self.phase == count:
            return (True, len(self.parts), 1, 0)
        stage = 2 * count - self.phase
        return (False, len(self.parts), self.stages[stage][0], stage)

    def accept(self, made):
        count = len(self.stages)
        if self.phase < count:
            size, stride = self.stages[self.phase]
            self.parts = [made[0]] + [with_peer(made[k], stride, k) for k in range(1, size)]
        elif self.phase < 2 * count:
            size, stride = self.stages[2 * count - 1 - self.phase]
            self.parts = [made[0]] + [with_peer(made[0], stride, k) for k in range(1, size)]
        else:
            self.parts = made
        self.phase += 1

    def last(self):
        return self.phase >= 2 * len(self.stages)


def advance(sums, digits, *ties):
    sums = [s for s in sums if not s.last()]
    if not sums:
        return ties
    jobs = [s.job() for s in sums]
    inputs, shapes, counts = [], [], []
    for s, (scatter, count, size, _) in zip(sums, jobs):
        rows, width = s.parts[0].shape
        inputs += s.parts
        made = [(rows // size, width)] * size if scatter else [(rows * size, width)]
        shapes += made
        counts.append(len(made))
    smem = pl.BlockSpec(memory_space=pltpu.SMEM)
    vmem = pl.BlockSpec(memory_space=pltpu.VMEM)
    outs = pl.pallas_call(
        functools.partial(local_kernel, jobs),
        out_shape=tuple(jax.ShapeDtypeStruct(shape, BF16) for shape in shapes),
        in_specs=[smem] + [vmem] * len(inputs),
        out_specs=(vmem,) * len(shapes),
        compiler_params=pltpu.CompilerParams(vmem_limit_bytes=VMEM_LIMIT),
        name="fold",
    )(digits, *inputs)
    outs, ties = lax.optimization_barrier((list(outs), ties))
    for s, count in zip(sums, counts):
        s.accept(outs[:count])
        outs = outs[count:]
    return ties


def unpack_kernel(layout, count, digit_ref, *refs):
    refs = list(refs)
    pieces = [[refs.pop(0) for _ in range(count)] for _ in range(2)]
    whole_two = refs.pop(0)
    up, down, inward, out, earth, small, hidden, entry, *joined = refs
    digit = digit_ref[0]
    for parts, whole in zip(pieces, joined):
        rows = parts[0].shape[0]
        for k, piece in enumerate(parts):
            whole[pl.ds(pl.multiple_of((digit ^ k) * rows, rows), rows), :] = piece[...]
    width = up.shape[1]
    hidden_part = up.shape[2]
    part = width // 2
    win = earth.shape[2]
    third = win // 3
    split = joined[0].shape[0]
    packs = [(joined[0], 0, joined[1], 0), (whole_two, 0, whole_two, split)]
    for b, (pack, base, other, base_other) in enumerate(packs):
        for at in range(0, hidden_part, width):
            low = base + at
            up[b, :, at : at + width] = pack[low : low + width, :].astype(F32)
            low += hidden_part
            down[b, at : at + width, :] = pack[low : low + width, :].T.astype(F32)

        def lines_of(place, start, size):
            low = base_other + place + start
            return other[low : low + size, :].astype(F32)

        for j in range(3):
            inward[b, j] = lines_of(layout.inward, j * part, part)
        out[b] = lines_of(layout.out, 0, part)
        rest = lines_of(layout.rest, 0, third)
        rest = jnp.concatenate([rest[:, k * 128 : (k + 1) * 128] for k in range(3)], axis=0)
        for k in range(earth.shape[1]):
            main = lines_of(layout.earth, (k // 3) * win, win)
            earth[b, k, :, :128] = main[:, (k % 3) * 128 : (k % 3 + 1) * 128]
            earth[b, k, :, 128:] = rest[:, k * (win - 128) : (k + 1) * (win - 128)]
        lines = lines_of(layout.small, 0, 16)
        small[b] = lines[:6]
        for j, at in enumerate(range(0, hidden_part, width)):
            hidden[b : b + 1, at : at + width] = lines[6 + j : 7 + j]
        last = lines[6 + hidden_part // width : 7 + hidden_part // width]
        entry[b, 0:1] = last[:, :part]
        entry[b, 1:2] = last[:, part:]


def unpack(digit, hidden_parts, attention_parts, whole_two, width, hidden_part, own_heads, win):
    vmem = pl.BlockSpec(memory_space=pltpu.VMEM)
    shapes = (
        (2, width, hidden_part),
        (2, hidden_part, width),
        (2, 3, width // 2, width),
        (2, width // 2, width),
        (2, own_heads, win, win),
        (2, 6, width),
        (2, hidden_part),
        (2, 2, width // 2),
    )
    count = len(hidden_parts)
    return pl.pallas_call(
        functools.partial(unpack_kernel, pack_rows(width, own_heads, win), count),
        out_shape=tuple(jax.ShapeDtypeStruct(shape, F32) for shape in shapes),
        in_specs=[pl.BlockSpec(memory_space=pltpu.SMEM)] + [vmem] * (2 * count + 1),
        out_specs=(vmem,) * len(shapes),
        scratch_shapes=[
            pltpu.VMEM((parts[0].shape[0] * count, width), BF16) for parts in (hidden_parts, attention_parts)
        ],
        compiler_params=pltpu.CompilerParams(vmem_limit_bytes=VMEM_LIMIT),
        name="unpack",
    )(digit, *hidden_parts, *attention_parts, whole_two)


def across(value):
    return lax.ppermute(value, TENSOR, [(0, 1), (1, 0)])


def local(
    tokens,
    token_mask,
    shift_next,
    cotangent,
    attend_gain,
    attend_shift,
    inward_weight,
    inward_bias,
    earth_bias,
    outward_weight,
    outward_bias,
    mixer_gain,
    mixer_shift,
    up_weight,
    up_bias,
    down_weight,
    down_bias,
):
    home, half, width = tokens.shape
    cap = home // 2
    part = lax.axis_index(TENSOR).astype(I32).reshape(1)
    tokens_oth = across(tokens)
    inward = jnp.transpose(inward_weight, (0, 2, 3, 1))
    own_heads = earth_bias.shape[1]
    hidden_part = up_weight.shape[2]
    win = 2 * half
    cotangent_oth = across(cotangent)
    meta, tab, place = make_plan(part, token_mask, shift_next, cap)
    common = dict(
        meta=meta,
        tab=tab,
        gain_one=attend_gain,
        shift_one=attend_shift,
        out_bias=outward_bias,
        gain_two=mixer_gain,
        shift_two=mixer_shift,
        down_bias=down_bias,
        entry_own=inward_bias,
        entry_oth=across(inward_bias),
        up_bias_own=up_bias,
        up_bias_oth=across(up_bias),
        in_own=inward,
        in_oth=across(inward),
        earth_own=earth_bias,
        earth_oth=across(earth_bias),
        out_own=outward_weight,
        out_oth=across(outward_weight),
        up_own=up_weight,
        up_oth=across(up_weight),
        down_own=down_weight,
        down_oth=across(down_weight),
    )
    sizes = (cap, half, width, own_heads, hidden_part)
    devices = lax.axis_size(DP)

    def run(stages, index, *more, split=(0, 1)):
        given = dict(common)
        for group in more:
            given.update(vars(group))
        return run_block(stages, index, Bag(**given), sizes, devices, split)

    rank = lax.axis_index(DP).astype(I32)
    digits, stride = [], 1
    for size in dp_groups(devices):
        digits.append(rank // stride % size)
        stride *= size
    digits = jnp.stack(digits)

    def sum_of(kernel):
        return DpSum([kernel.pack_own, across(kernel.pack_oth)])

    first = Bag(src=tokens, src_oth=tokens_oth)
    ahead_one = run((True, False, False), 0, first)
    second = Bag(src=ahead_one.out, src_oth=across(ahead_one.out_half))
    mixer_two = run((True, True, False), 1, second, Bag(grad_src=cotangent, grad_oth=cotangent_oth))
    pack_far = across(mixer_two.pack_oth)
    recv_b = across(mixer_two.send)
    attention_two = run((False, False, True), 1, mixer_two, second)
    half_far = across(attention_two.out_half)
    pack_two = stack((mixer_two.pack_own, pack_far), (attention_two.pack_own, across(attention_two.pack_oth)))
    pack_two, half_far = lax.optimization_barrier((pack_two, half_far))
    sum_two = lax.psum(pack_two, DP)
    back = Bag(grad_src=attention_two.out, grad_oth=half_far)
    mixer_one = run((False, True, False), 0, ahead_one, first, back)
    sum_mixer_one = sum_of(mixer_one)
    (do,) = advance([sum_mixer_one], digits, mixer_one.do)
    halves, across_one = [], []
    for which in range(PARTS):
        if which:
            (do,) = advance([sum_mixer_one], digits, do)
        halves.append(run((False, False, True), 0, ahead_one, mixer_one, Bag(do=do), first, split=(which, PARTS)))
        across_one.append(across(halves[-1].pack_oth))
    sum_attention_one = DpSum([half_of.pack_own for half_of in halves] + across_one)
    recv_a = [across(half_of.send) for half_of in halves]
    sums = [sum_mixer_one, sum_attention_one]
    while not all(s.last() for s in sums):
        advance(sums, digits)
    tokens_grad, block_output = settle(
        place, [half_of.keep for half_of in halves] + recv_a, [mixer_two.keep, recv_b]
    )
    g_up, g_down, g_in, g_out, g_earth, small, hidden, entry = unpack(
        digits[:1], sum_mixer_one.parts, sum_attention_one.parts, sum_two, width, hidden_part, own_heads, win
    )
    return (
        block_output,
        tokens_grad,
        small[:, 0],
        small[:, 1],
        jnp.transpose(g_in, (0, 3, 1, 2)),
        entry,
        g_earth,
        g_out,
        small[:, 2],
        small[:, 3],
        small[:, 4],
        g_up,
        hidden,
        g_down,
        small[:, 5],
    )


def solution(mesh):
    placed = (
        P(DP, TENSOR, None),
        P(DP, None),
        P(DP),
        P(DP, TENSOR, None),
        P(),
        P(),
        P(None, None, None, TENSOR),
        P(None, None, TENSOR),
        P(None, TENSOR, None, None),
        P(None, TENSOR, None),
        P(),
        P(),
        P(),
        P(None, None, TENSOR),
        P(None, TENSOR),
        P(None, TENSOR, None),
        P(),
    )
    return jax.shard_map(
        local,
        mesh=mesh,
        in_specs=placed,
        out_specs=(
            P(DP, TENSOR, None),
            P(DP, TENSOR, None),
            P(),
            P(),
            P(None, None, None, TENSOR),
            P(None, None, TENSOR),
            P(None, TENSOR, None, None),
            P(None, TENSOR, None),
            P(),
            P(),
            P(),
            P(None, None, TENSOR),
            P(None, TENSOR),
            P(None, TENSOR, None),
            P(),
        ),
        check_vma=False,
    )
```

```python
import functools
from types import SimpleNamespace as Bag

import jax
import jax.numpy as jnp
from jax import lax
from jax.experimental import pallas as pl
from jax.experimental.pallas import tpu as pltpu
from jax.sharding import PartitionSpec as P

F32 = jnp.float32
BF16 = jnp.bfloat16
I32 = jnp.int32

CHUNK = 4
TILE = 4
DP = "dp"
TENSOR = "tensor"
LATS = 6
HALF_COLS = 6
COST_CUT = 64
PARTS = 1
LN2 = 0.6931471805599453
NEVER = -1000000000.0
VMEM_LIMIT = 60 * 1024 * 1024


def mm(a, b):
    return lax.dot_general(a, b, (((1,), (0,)), ((), ())), preferred_element_type=F32)


def mm_nt(a, b):
    return lax.dot_general(a, b, (((1,), (1,)), ((), ())), preferred_element_type=F32)


def mm_tn(a, b):
    return lax.dot_general(a, b, (((0,), (0,)), ((), ())), preferred_element_type=F32)


def fold_rows(values):
    rows, width = values.shape
    return jnp.sum(values.reshape(rows // 8, 8, width), axis=0)


def plan_kernel(t_ref, mask_ref, next_ref, meta_ref, tab_ref, place_ref, seen, order, first, last, rows, cols):
    home = next_ref.shape[0]
    cap = tab_ref.shape[1]
    half = mask_ref.shape[1] // 2
    t = t_ref[0]

    def clear(s, carry):
        seen[s] = 0
        place_ref[0, s] = -1
        place_ref[1, s] = -1
        high = mask_ref[s, 0]
        for i in range(1, LATS):
            high += mask_ref[s, i * HALF_COLS]
        wide = mask_ref[s, 0] + mask_ref[s, half]
        for j in range(1, HALF_COLS):
            wide += mask_ref[s, j] + mask_ref[s, half + j]
        rows[s] = high
        cols[s] = wide
        return carry

    lax.fori_loop(0, home, clear, 0)

    def visit(origin, count):
        fresh = (rows[origin] > 0) & (seen[origin] == 0)

        def walk(carry):
            s, at, _ = carry
            seen[s] = 1
            order[at] = s
            first[at] = count
            following = next_ref[s]
            return following, at + 1, (following != origin) & (at + 1 < home)

        return lax.while_loop(lambda carry: carry[2], walk, (origin, count, fresh))[1]

    total = lax.fori_loop(0, home, visit, 0)

    def close(back, carry):
        p = total - 1 - back
        after = jnp.minimum(p + 1, home - 1)
        ends = (p == total - 1) | (first[after] != first[p])
        end = jnp.where(ends, p, carry)
        last[p] = end
        return end

    lax.fori_loop(0, total, close, 0)

    cut = (total + 1) // 2
    base = t * cut
    n = jnp.where(t == 0, cut, total - cut)

    def fill(i, carry):
        live = i < n
        p = jnp.where(live, base + i, 0)
        slot = jnp.where(live, order[p], 0)
        ahead = jnp.where(p == last[p], first[p], p + 1)
        behind = jnp.where(p == first[p], last[p], p - 1)
        next_slot = next_ref[slot]
        ahead_in = live & (ahead >= base) & (ahead < base + n)
        behind_in = live & (behind >= base) & (behind < base + n)
        tab_ref[0, i] = slot
        tab_ref[1, i] = jnp.where(ahead_in, ahead - base, -1)
        tab_ref[2, i] = jnp.where(behind_in, behind - base, -1)
        tab_ref[3, i] = jnp.where(live, rows[slot], 0)
        tab_ref[4, i] = jnp.where(live, cols[slot], 0)
        tab_ref[5, i] = jnp.where(live, rows[next_slot], 0)
        tab_ref[6, i] = jnp.where(live, cols[next_slot], 0)
        tab_ref[7, i] = jnp.where(live, next_slot, 0)
        return carry

    @pl.when(total == 0)
    def _():
        order[0] = 0
        first[0] = 0
        last[0] = 0

    lax.fori_loop(0, cap, fill, 0)

    def settle(p, carry):
        slot = order[p]
        owner = jnp.where(p >= cut, 1, 0)
        here = p - owner * cut
        source = jnp.where(owner == t, here, cap + here)
        place_ref[0, slot] = source
        place_ref[1, jnp.where(t == 1, slot, next_ref[slot])] = source
        return carry

    lax.fori_loop(0, total, settle, 0)

    crossing = (cut < total) & (first[jnp.minimum(cut, home - 1)] < cut)
    tail = jnp.maximum(cut - 1, 0)
    meta_ref[0] = n
    meta_ref[1] = jnp.where(crossing & (t == 0), first[jnp.minimum(cut, home - 1)], 0)
    meta_ref[2] = jnp.where(t == 0, tail, jnp.where(crossing, last[tail] - cut, 0))
    meta_ref[3] = t
    for spare in range(4, 8):
        meta_ref[spare] = 0


def make_plan(part, token_mask, shift_next, cap):
    home = shift_next.shape[0]
    smem = pl.BlockSpec(memory_space=pltpu.SMEM)
    return pl.pallas_call(
        plan_kernel,
        out_shape=(
            jax.ShapeDtypeStruct((8,), I32),
            jax.ShapeDtypeStruct((8, cap), I32),
            jax.ShapeDtypeStruct((2, home), I32),
        ),
        in_specs=[smem, smem, smem],
        out_specs=(smem, smem, smem),
        scratch_shapes=[pltpu.SMEM((home,), I32) for _ in range(6)],
        cost_estimate=pl.CostEstimate(flops=5 * 10**9, bytes_accessed=2**24, transcendentals=0),
        name="plan",
    )(part, token_mask, shift_next)


def gelu_pair(u):
    cdf = 0.5 + 0.5 * lax.erf(u * 0.7071067811865476)
    return u * cdf, cdf + u * (0.3989422804014327 * jnp.exp(-0.5 * (u * u)))


def normalise(values):
    centred = values - jnp.mean(values, axis=-1, keepdims=True)
    spread = jnp.mean(centred * centred, axis=-1, keepdims=True)
    scale = lax.rsqrt(spread + 1e-05)
    return centred * scale, scale


def norm_back(grad, unit, scale, gain):
    inner = grad * gain
    mean_one = jnp.mean(inner, axis=-1, keepdims=True)
    mean_two = jnp.mean(inner * unit, axis=-1, keepdims=True)
    return scale * (inner - mean_one - unit * mean_two)


def block_kernel(names, stages, index, head_width, span_of, *refs):
    ref = Bag(**dict(zip(names, refs, strict=True)))
    ahead, mixer, attention = stages
    if ahead or attention:
        in_sides = (ref.in_own, ref.in_oth)
    if ahead or mixer:
        out_sides, up_sides, down_sides = ((ref.out_own, ref.out_oth), (ref.up_own, ref.up_oth), (ref.down_own, ref.down_oth))
    if ahead:
        earth_sides, entry_sides = (ref.earth_own, ref.earth_oth), (ref.entry_own, ref.entry_oth)
        up_bias_sides = (ref.up_bias_own, ref.up_bias_oth)
    if mixer or attention:
        pack_sides = (ref.pack_own, ref.pack_oth)
    shifted = index == 1
    meta, tab = ref.meta, ref.tab
    cap = tab.shape[1]
    half, width = ref.xs.shape[2:]
    win = 2 * half
    rows_all = CHUNK * win
    part = width // 2
    groups = width // 128
    per_group = 128 // head_width
    heads = width // head_width
    own_heads = heads // 2
    scale = head_width**-0.5
    n = meta[0]
    t = meta[3]
    lead, span_count = span_of
    step = pl.program_id(0)
    w0 = lead + step * CHUNK
    first_step = step == 0
    lanes = lax.broadcasted_iota(I32, (1, 128), 1) // head_width
    head_keep = [jnp.where(lanes == k, 1.0, 0.0).astype(BF16) for k in range(per_group)]
    lane = lax.broadcasted_iota(I32, (win, 128), 1)
    spots = [((u + 1) % per_group) * head_width for u in range(per_group)]
    spare_lane = [lane == spot for spot in spots]
    spare_two = [(lane == spot) | (lane == spot + 1) for spot in spots]
    one = jnp.ones((), BF16)
    pitch = -(-win // 256) * 256
    blank_lanes = jnp.zeros((win, pitch - win), BF16)
    blank_rows = jnp.zeros((pitch - win, 128), BF16)
    wide_step = TILE * win

    def row(table):
        return table[index : index + 1, :]

    def by_part(west, one_ref, other, at, dst, sem):
        is_own = t == (0 if west else 1)

        @pl.when(is_own)
        def _():
            pltpu.make_async_copy(one_ref.at[at], dst, sem).start()

        @pl.when(jnp.logical_not(is_own))
        def _():
            pltpu.make_async_copy(other.at[at], dst, sem).start()

    def by_place(local, local_half, one_ref, other, dst, sem):
        @pl.when(local >= 0)
        def _():
            pltpu.make_async_copy(one_ref.at[local, local_half], dst, sem).start()

        @pl.when(local < 0)
        def _():
            pltpu.make_async_copy(other, dst, sem).start()

    xs, x_sem = ref.xs, ref.x_sem
    if mixer:
        rs, r_sem = ref.rs, ref.r_sem

    if ahead:
        bias_copies = [
            pltpu.make_async_copy(
                side.at[index], ref.bias.at[pl.ds(s * own_heads, own_heads)], ref.b_sem.at[s]
            )
            for s, side in enumerate(earth_sides)
        ]

    @pl.when(first_step)
    def _():
        if ahead:
            for copy in bias_copies:
                copy.start()

        def start_loads(i, carry):
            if shifted:
                by_place(i, 1, ref.src, ref.src_oth, xs.at[i, 0], x_sem.at[i, 0])
                by_place(tab[1, i], 0, ref.src, ref.src_oth, xs.at[i, 1], x_sem.at[i, 1])
            else:
                by_part(True, ref.src, ref.src_oth, tab[0, i], xs.at[i, 0], x_sem.at[i, 0])
                by_part(False, ref.src, ref.src_oth, tab[0, i], xs.at[i, 1], x_sem.at[i, 1])
            if mixer and shifted:
                by_part(False, ref.grad_src, ref.grad_oth, tab[0, i], rs.at[i, 0], r_sem.at[i, 0])
                by_part(True, ref.grad_src, ref.grad_oth, tab[7, i], rs.at[i, 1], r_sem.at[i, 1])
            elif mixer:
                by_place(tab[2, i], 1, ref.grad_src, ref.grad_oth, rs.at[i, 0], r_sem.at[i, 0])
                by_place(i, 0, ref.grad_src, ref.grad_oth, rs.at[i, 1], r_sem.at[i, 1])
            return carry

        lax.fori_loop(lead, jnp.minimum(lead + span_count, n), start_loads, 0)

        def blank(i, carry):
            for k in range(2):
                xs[i, k] = jnp.zeros_like(xs[i, k])
                if mixer:
                    rs[i, k] = jnp.zeros_like(rs[i, k])
            return carry

        lax.fori_loop(jnp.maximum(n, lead), lead + span_count, blank, 0)
        if mixer:
            from_head = lax.broadcasted_iota(I32, (width, width), 0) // head_width
            to_head = lax.broadcasted_iota(I32, (width, width), 1) // head_width
            same = from_head // per_group == to_head // per_group
            following = (from_head + 1) % per_group == to_head % per_group
            ref.spread[...] = jnp.where(same & following, 1.0, 0.0).astype(BF16)
        if ahead or attention:
            for j in range(3):
                for s, side in enumerate(in_sides):
                    at = j * width + s * part
                    ref.w_in[at : at + part, :] = side[j]
        if ahead or mixer:
            for s, side in enumerate(out_sides):
                ref.wo[s * part : (s + 1) * part, :] = side[...]
            level = LATS * HALF_COLS
            place = lax.broadcasted_iota(I32, (win, 128), 0)
            inside = place
            for bound in (level, 2 * level, 3 * level):
                inside = inside - jnp.where(place >= bound, level, 0)
            lat = jnp.zeros_like(inside)
            for bound in range(HALF_COLS, level, HALF_COLS):
                lat = lat + jnp.where(inside >= bound, 1, 0)
            ref.lat[...] = lat
            ref.col[...] = inside - HALF_COLS * lat
        if ahead:
            for copy in bias_copies:
                copy.wait()
            for k in range(heads):
                ref.bias[k] = ref.bias[k] * (1.0 / LN2)
        sums = [ref.acc_small] if mixer or attention else []
        if mixer:
            sums += [ref.acc_up, ref.acc_down, ref.acc_out, ref.acc_hidden]
        if attention:
            sums += [ref.acc_in, ref.acc_earth, ref.acc_entry]
        for table in sums:
            table[...] = jnp.zeros_like(table)

    def extents(i):
        high, wide, high_next, wide_next = tab[3, i], tab[4, i], tab[5, i], tab[6, i]
        if shifted:
            return (high, wide - HALF_COLS), (high_next, wide_next)
        return (high, wide), (high, wide - HALF_COLS)

    def valid_rows(i, k):
        high, wide = extents(i)[k]
        valid = (ref.lat[:half] < high) & (ref.col[:half] < wide)
        return jnp.concatenate([jnp.where(valid, 1.0, 0.0)] * groups, axis=1)

    def tile_x(tile):
        parts = []
        for j in range(TILE):
            for k in range(2):
                parts.append(xs[w0 + tile * TILE + j, k].astype(F32))
        return jnp.concatenate(parts, axis=0)

    def entrance(tile, c):
        rows = pl.ds(pl.multiple_of(tile * wide_step, wide_step), wide_step)
        unit, _ = normalise(tile_x(tile))
        low = (unit * row(ref.gain_one) + row(ref.shift_one)).astype(BF16)
        ref.h1[rows, :] = low
        for j in range(3):
            cols = slice(j * width, (j + 1) * width)
            value = mm_nt(low, ref.w_in[cols, :])
            if j != 1:
                value = value + jnp.concatenate(
                    [side[index, j // 2 : j // 2 + 1, :] for side in entry_sides], axis=1
                )
            if j == 0:
                value = value * (scale / LN2)
            ref.qkv[rows, cols] = value.astype(BF16)
        return c

    def attend(pair, c):
        for j in range(2):
            attend_one(pair * 2 + j)
        return c

    def attend_one(w):
        rows = pl.ds(pl.multiple_of(w * win, win), win)
        (high_a, wide_a), (high_b, wide_b) = extents(w0 + w)
        west = lax.broadcasted_iota(I32, (win, 128), 0) < half
        high = jnp.where(west, high_a, high_b)
        wide = jnp.where(west, wide_a, wide_b)
        hide = jnp.where((ref.lat[...] < high) & (ref.col[...] < wide), 0.0, NEVER).astype(BF16)
        for g in range(groups):
            span = [slice(j * width + g * 128, j * width + (g + 1) * 128) for j in range(3)]
            q, k, v = (ref.qkv[rows, cols] for cols in span)
            total = []
            for u in range(per_group):
                head = g * per_group + u
                spare = spare_lane[u]
                s = mm_nt(jnp.where(spare, one, q * head_keep[u]), jnp.where(spare, hide, k))
                s = s + ref.bias[head]
                low = jnp.exp2(s - jnp.max(s, axis=-1, keepdims=True)).astype(BF16)
                ref.probs[w, head] = low
                total.append(jnp.concatenate([low, blank_lanes], axis=1))
            tall = [value for keep in head_keep for value in (v * keep, blank_rows)]
            ones = [value for keep in head_keep for value in (jnp.broadcast_to(keep, (win, 128)), blank_rows)]
            tall = jnp.concatenate([jnp.concatenate(tall, axis=0), jnp.concatenate(ones, axis=0)], axis=1)
            total = mm(jnp.concatenate(total, axis=1), tall)
            inverse = 1.0 / total[:, 128:]
            cols = slice(g * 128, (g + 1) * 128)
            ref.att[rows, cols] = (total[:, :128] * inverse).astype(BF16)
            ref.inverse[rows, cols] = inverse.astype(BF16)

    hidden_part = up_sides[0].shape[1] if ahead or mixer else 0
    hidden = 2 * hidden_part
    pieces = [(s, at) for s in range(2) for at in range(0, hidden_part, 384)]

    def middle(tile, c):
        rows = pl.ds(pl.multiple_of(tile * wide_step, wide_step), wide_step)
        att = ref.att[rows, :]
        v2 = tile_x(tile) + mm(att, ref.wo[...]) + row(ref.out_bias)
        unit, unit_scale = normalise(v2)
        if ahead:
            low = (unit * row(ref.gain_two) + row(ref.shift_two)).astype(BF16)
            ref.h2[rows, :] = low
            result = v2 + row(ref.down_bias)
        if mixer:
            parts = []
            for j in range(TILE):
                i = w0 + tile * TILE + j
                for k in range(2):
                    r = rs[i, k].astype(F32)
                    if shifted:
                        r = r * valid_rows(i, k)
                    parts.append(r)
            r = jnp.concatenate(parts, axis=0)
            r_low = r.astype(BF16)
            ref.rr[rows, :] = r_low
        for s, off in pieces:
            cols = slice(off, off + 384)
            at = off + s * hidden_part
            span = slice(at, at + 384)
            if ahead:
                u = mm(low, up_sides[s][:, cols]) + up_bias_sides[s][index : index + 1, cols]
                g, slope = gelu_pair(u)
                g = g.astype(BF16)
                ref.act[rows, span] = g
                if not mixer:
                    ref.slope[rows, span] = slope.astype(BF16)
            else:
                slope = ref.slope[rows, span].astype(F32)
            if mixer:
                du = mm_nt(r_low, down_sides[s][cols, :]) * slope
                ref.acc_hidden[:, span] += fold_rows(du)
                du = du.astype(BF16)
                ref.du[rows, span] = du
        sides = [slice(s * hidden_part, (s + 1) * hidden_part) for s in range(2)]
        if ahead:
            for side, cols in zip(down_sides, sides):
                result = result + mm(ref.act[rows, cols], side[...])
        if mixer:
            d_h2 = mm_nt(ref.du[rows, sides[0]], up_sides[0][...]) + mm_nt(ref.du[rows, sides[1]], up_sides[1][...])
        if ahead:
            for j in range(TILE):
                i = w0 + tile * TILE + j
                for k in range(2):
                    at = j * win + k * half
                    piece = result[at : at + half]
                    if not shifted:
                        ref.out[i, k] = piece.astype(BF16)
                        continue
                    piece = (piece * valid_rows(i, k)).astype(BF16)
                    place_half(ref.keep, ref.send, i, 1 - k, piece)
        if mixer:
            ref.acc_small[5] += fold_rows(r)
            ref.acc_small[4] += fold_rows(d_h2)
            ref.acc_small[3] += fold_rows(d_h2 * unit)
            dv2 = r + norm_back(d_h2, unit, unit_scale, row(ref.gain_two))
            ref.acc_small[2] += fold_rows(dv2)
            da = dv2.astype(BF16)
            ref.da[rows, :] = da
            d_att = mm_nt(da, ref.wo[...]) * ref.inverse[rows, :].astype(F32)
            ref.do[rows, :] = d_att.astype(BF16)
            inner = (d_att * att.astype(F32)).astype(BF16)
            delta = -mm(inner, ref.spread[...])
            high = delta.astype(BF16)
            rest = (delta - high.astype(F32)).astype(BF16)
            spot = lax.broadcasted_iota(I32, (1, width), 1) % head_width
            ref.aug[rows, :] = jnp.where(spot == 0, high, jnp.where(spot == 1, rest, jnp.zeros_like(rest)))
        return c

    def place_half(keep, send, i, owner, piece):
        @pl.when(t == owner)
        def _():
            keep[i] = piece

        @pl.when(t != owner)
        def _():
            send[i] = piece

    def hidden_grads(_, c):
        r_turned = ref.rr[...].T
        h_turned = ref.h2[...].T
        for at in range(0, hidden, 256):
            cols = slice(at, at + 256)
            ref.acc_down[:, cols] += mm(r_turned, ref.act[:, cols])
            ref.acc_up[:, cols] += mm(h_turned, ref.du[:, cols])
        ref.acc_out[...] += mm(ref.att[...].T, ref.da[...])
        return c

    def attend_back(pair, c):
        spans = [pl.ds(pl.multiple_of((pair * 2 + j) * win, win), win) for j in range(2)]
        for g in range(groups):
            span = [slice(j * width + g * 128, j * width + (g + 1) * 128) for j in range(3)]
            here = slice(g * 128, (g + 1) * 128)
            loaded = []
            for rows in spans:
                q, k, v = (ref.qkv[rows, cols] for cols in span)
                dog = ref.do[rows, here]
                loaded.append((q.T, k, v, dog, dog.T, ref.aug[rows, here], [], [], []))
            for u in range(per_group):
                head = g * per_group + u
                cut = slice(u * head_width, (u + 1) * head_width)
                total = None
                for j in range(2):
                    q_turned, k, v, dog, do_turned, augment, dq, dk, dv = loaded[j]
                    low = ref.probs[pair * 2 + j, head]
                    dom = jnp.where(spare_two[u], augment, dog * head_keep[u])
                    dp = mm_nt(dom, jnp.where(spare_two[u], one, v))
                    ds = low.astype(F32) * dp
                    total = ds if total is None else total + ds
                    ds = ds.astype(BF16)
                    dk.append(mm(q_turned[cut], ds))
                    dv.append(mm(do_turned[cut], low))
                    dq.append(jnp.concatenate([ds, blank_lanes], axis=1))
                ref.acc_earth[head] += total
            for j, rows in enumerate(spans):
                dq, dk, dv = loaded[j][6:]
                k = loaded[j][1]
                tall = [value for keep in head_keep for value in (k * keep, blank_rows)]
                dq = mm(jnp.concatenate(dq, axis=1), jnp.concatenate(tall, axis=0)) * scale
                dk = (jnp.concatenate(dk, axis=0) * LN2).T
                dv = jnp.concatenate(dv, axis=0).T
                for at, value in ((0, dq), (2, dv)):
                    ref.acc_entry[:, span[at]] += fold_rows(value)
                for at, value in enumerate((dq, dk, dv)):
                    ref.dqkv[rows, span[at]] = value.astype(BF16)
        return c

    def exit_back(tile, c):
        rows = pl.ds(pl.multiple_of(tile * wide_step, wide_step), wide_step)
        unit, unit_scale = normalise(tile_x(tile))
        dh = mm(ref.dqkv[rows, :], ref.w_in[...])
        ref.acc_small[1] += fold_rows(dh)
        ref.acc_small[0] += fold_rows(dh * unit)
        dv = ref.da[rows, :].astype(F32) + norm_back(dh, unit, unit_scale, row(ref.gain_one))
        for j in range(TILE):
            i = w0 + tile * TILE + j
            for k in range(2):
                at = j * win + k * half
                piece = dv[at : at + half].astype(BF16)
                if shifted:
                    ref.out[i, k] = piece
                else:
                    place_half(ref.keep, ref.send, i - lead, k, piece)
        return c

    def weight_grads(_, c):
        turned = ref.h1[...].T
        for j in range(3):
            cols = slice(j * width, (j + 1) * width)
            ref.acc_in[:, cols] += mm(turned, ref.dqkv[:, cols])
        return c

    @pl.when(w0 < n)
    def _():
        def wait_loads(i, c):
            for k in range(2):
                pltpu.make_async_copy(xs.at[i, k], xs.at[i, k], x_sem.at[i, k]).wait()
                if mixer:
                    pltpu.make_async_copy(rs.at[i, k], rs.at[i, k], r_sem.at[i, k]).wait()
            return c

        lax.fori_loop(w0, jnp.minimum(w0 + CHUNK, n), wait_loads, 0)
        if ahead:
            lax.fori_loop(0, CHUNK // TILE, entrance, 0)
            lax.fori_loop(0, CHUNK // 2, attend, 0)
        if ahead or mixer:
            lax.fori_loop(0, CHUNK // TILE, middle, 0)
        if mixer:
            lax.fori_loop(0, 1, hidden_grads, 0)
        if attention:
            lax.fori_loop(0, CHUNK // 2, attend_back, 0)
            lax.fori_loop(0, CHUNK // TILE, exit_back, 0)
            lax.fori_loop(0, 1, weight_grads, 0)

    @pl.when(step == pl.num_programs(0) - 1)
    def _():
        if ahead and not shifted:
            ref.out_half[...] = ref.out[meta[1], 0]
        if attention and shifted:
            ref.out_half[...] = ref.out[meta[2], 1]
        if mixer:
            for s, pack in enumerate(pack_sides):
                base = s * hidden_part
                for at in range(0, hidden_part, width):
                    cols = slice(base + at, base + at + width)
                    pack[at : at + width, :] = ref.acc_up[:, cols].astype(BF16)
                    pack[hidden_part + at : hidden_part + at + width, :] = ref.acc_down[:, cols].astype(BF16)
                low, high = 2 * hidden_part, 2 * hidden_part + part
                pack[low:high, :] = ref.acc_out[s * part : (s + 1) * part, :].astype(BF16)
                if pack.shape[0] > high:
                    pack[high:, :] = jnp.zeros_like(pack[high:, :])
            ref.sums_small[...] = jnp.sum(ref.acc_small[...], axis=1)
            ref.sums_hidden[...] = jnp.sum(ref.acc_hidden[...], axis=0, keepdims=True)
        if attention:
            small = jnp.sum(ref.acc_small[...], axis=1)
            hidden_sum = ref.sums_hidden[...]
            if lead == 0:
                small = small + ref.sums_small[...]
            else:
                hidden_sum = jnp.zeros_like(hidden_sum)
            half_hidden = hidden_sum.shape[1] // 2
            entry_sum = jnp.sum(ref.acc_entry[...], axis=0, keepdims=True)
            layout = pack_rows(width, own_heads, win)
            for s, pack in enumerate(pack_sides):
                cuts = [slice(j * width + s * part, j * width + (s + 1) * part) for j in range(3)]
                for j, cut in enumerate(cuts):
                    at = layout.inward + j * part
                    pack[at : at + part, :] = ref.acc_in[:, cut].T.astype(BF16)
                earth = [ref.acc_earth[s * own_heads + k] for k in range(own_heads)]
                for k, value in enumerate(earth):
                    row_at = layout.earth + (k // 3) * win
                    pack[row_at : row_at + win, (k % 3) * 128 : (k % 3 + 1) * 128] = value[:, :128].astype(BF16)
                rest = jnp.concatenate([value[:, 128:] for value in earth], axis=1)
                rest = jnp.concatenate([rest, jnp.zeros((win, 128 - rest.shape[1]), F32)], axis=1)
                third = win // 3
                for k in range(3):
                    pack[layout.rest : layout.rest + third, k * 128 : (k + 1) * 128] = rest[
                        k * third : (k + 1) * third
                    ].astype(BF16)
                lines = [small]
                for at in range(s * half_hidden, (s + 1) * half_hidden, width):
                    lines.append(hidden_sum[:, at : at + width])
                lines.append(jnp.concatenate([entry_sum[:, cuts[0]], entry_sum[:, cuts[2]]], axis=1))
                count = small.shape[0] + len(lines) - 1
                lines.append(jnp.zeros((16 - count, width), F32))
                pack[layout.small : layout.small + 16, :] = jnp.concatenate(lines, axis=0).astype(BF16)
                if pack.shape[0] > layout.total:
                    pack[layout.total :, :] = jnp.zeros_like(pack[layout.total :, :])


def pack_rows(width, own_heads, win):
    counts = dict(
        inward=3 * width // 2, earth=own_heads // 3 * win, rest=win // 3, small=16, total=0
    )
    layout, at = {}, 0
    for name, count in counts.items():
        layout[name] = at
        at += count
    return Bag(**layout)


def padded(rows, devices):
    unit = 16 * devices
    return -(-rows // unit) * unit


def run_block(stages, index, given, sizes, devices, split):
    cap, half, width, own_heads, hidden_part = sizes
    ahead, mixer, attention = stages
    shifted = index == 1
    win = 2 * half
    rows = CHUNK * win
    heads = 2 * own_heads
    hidden = 2 * hidden_part
    head_width = width // heads
    which, parts = split
    steps = cap // CHUNK // parts
    lead = which * steps * CHUNK
    smem = pl.BlockSpec(memory_space=pltpu.SMEM)
    hbm = pl.BlockSpec(memory_space=pl.ANY)
    ins, outs, scratch = {}, {}, {}

    def whole(shape):
        zeros = (0,) * len(shape)
        return pl.BlockSpec(shape, lambda c: zeros, pipeline_mode=pl.Buffered(1))

    def take(spec, **arrays):
        for name, array in arrays.items():
            ins[name] = (array, whole(array.shape) if spec is None else spec)

    def take_block(**arrays):
        for name, array in arrays.items():
            at = (index,) + (0,) * (array.ndim - 1)
            spec = pl.BlockSpec((None,) + array.shape[1:], lambda c, at=at: at, pipeline_mode=pl.Buffered(1))
            ins[name] = (array, spec)

    def chunked(shape):
        zeros = (0,) * (len(shape) - 1)
        return pl.BlockSpec(shape, lambda c: (which * steps + c,) + zeros)

    def give(dtype=BF16, **shapes):
        for name, shape in shapes.items():
            outs[name] = (jax.ShapeDtypeStruct(shape, dtype), whole(shape))

    flat = lambda factor: (rows, factor * width)
    stash = dict(
        qkv=flat(3),
        probs=(CHUNK, heads, win, win),
        att=flat(1),
        inverse=flat(1),
        h1=flat(1),
        h2=flat(1),
        act=(rows, hidden),
        slope=(rows, hidden),
        da=flat(1),
        do=flat(1),
        aug=flat(1),
    )

    def carry_in(**arrays):
        for name, array in arrays.items():
            ins[name] = (array, chunked(stash[name]))

    def carry_out(**wanted):
        for name in wanted:
            shape = stash[name]
            full = jax.ShapeDtypeStruct((shape[0] * cap // CHUNK,) + shape[1:], BF16)
            outs[name] = (full, chunked(shape))

    g = given
    take(smem, meta=g.meta, tab=g.tab)
    take(hbm, src=g.src, src_oth=g.src_oth)
    if mixer:
        take(hbm, grad_src=g.grad_src, grad_oth=g.grad_oth)
    if ahead:
        take(hbm, earth_own=g.earth_own, earth_oth=g.earth_oth)
        take(None, shift_one=g.shift_one, shift_two=g.shift_two, down_bias=g.down_bias)
        take(None, entry_own=g.entry_own, entry_oth=g.entry_oth)
        take(None, up_bias_own=g.up_bias_own, up_bias_oth=g.up_bias_oth)
    if ahead or mixer:
        take(None, out_bias=g.out_bias, gain_two=g.gain_two)
        take_block(out_own=g.out_own, out_oth=g.out_oth, up_own=g.up_own, up_oth=g.up_oth)
        take_block(down_own=g.down_own, down_oth=g.down_oth)
    if ahead or attention:
        take(None, gain_one=g.gain_one)
        take_block(in_own=g.in_own, in_oth=g.in_oth)
    if attention:
        take(None, sums_small=g.sums_small, sums_hidden=g.sums_hidden)
        carry_in(qkv=g.qkv, probs=g.probs, h1=g.h1, da=g.da, do=g.do, aug=g.aug)
    elif not ahead:
        carry_in(att=g.att, inverse=g.inverse, h2=g.h2, act=g.act, slope=g.slope)

    half_shape = (half, width)
    if ahead:
        carry_out(qkv=1, probs=1, att=1, h1=1)
        if not mixer:
            carry_out(inverse=1, h2=1, act=1, slope=1)
    if mixer:
        carry_out(da=1, do=1, aug=1)
    if (ahead and not shifted) or (attention and shifted):
        give(out=(cap, 2) + half_shape, out_half=half_shape)
    if (ahead and shifted) or (attention and not shifted):
        give(keep=(cap // parts,) + half_shape, send=(cap // parts,) + half_shape)
    if mixer:
        pack = (padded(2 * hidden_part + width // 2, devices), width)
        give(pack_own=pack, pack_oth=pack)
        give(F32, sums_small=(6, width), sums_hidden=(1, hidden))
    if attention:
        pack = (padded(pack_rows(width, own_heads, win).total, devices), width)
        give(pack_own=pack, pack_oth=pack)

    def hold(dtype=BF16, **shapes):
        for name, shape in shapes.items():
            scratch[name] = pltpu.VMEM(shape, dtype)

    halves = (cap, 2) + half_shape
    hold(xs=halves)
    scratch.update(x_sem=pltpu.SemaphoreType.DMA((cap, 2)))
    if ahead:
        hold(F32, bias=(heads, win, win))
        scratch.update(b_sem=pltpu.SemaphoreType.DMA((2,)))
    if ahead or attention:
        hold(w_in=(3 * width, width))
    if ahead or mixer:
        hold(wo=(width, width))
        hold(I32, lat=(win, 128), col=(win, 128))
    if ahead and mixer:
        hold(inverse=flat(1), h2=flat(1), act=(rows, hidden))
    if mixer:
        hold(rs=halves, rr=flat(1), du=(rows, hidden), spread=(width, width))
        scratch.update(r_sem=pltpu.SemaphoreType.DMA((cap, 2)))
        hold(F32, acc_up=(width, hidden), acc_down=(width, hidden), acc_hidden=(8, hidden), acc_out=(width, width))
    if attention:
        hold(dqkv=flat(3))
        hold(F32, acc_in=(width, 3 * width), acc_earth=(heads, win, win))
        hold(F32, acc_entry=(8, 3 * width))
    if mixer or attention:
        hold(F32, acc_small=(6, 8, width))

    matmuls = cap * win * (4 * width * width + 2 * width * hidden)
    result = pl.pallas_call(
        functools.partial(
            block_kernel, [*ins, *outs, *scratch], stages, index, head_width, (lead, steps * CHUNK)
        ),
        grid=(steps,),
        out_shape=tuple(shape for shape, _ in outs.values()),
        in_specs=[spec for _, spec in ins.values()],
        out_specs=tuple(spec for _, spec in outs.values()),
        scratch_shapes=list(scratch.values()),
        compiler_params=pltpu.CompilerParams(vmem_limit_bytes=VMEM_LIMIT),
        cost_estimate=pl.CostEstimate(
            flops=2 * sum(stages) * matmuls // COST_CUT,
            bytes_accessed=8 * sum(stages) * cap * win * width * 2 // COST_CUT,
            transcendentals=cap * win * hidden // COST_CUT,
        ),
        name=("ahead" if ahead else "") + ("mixer" if mixer else "") + ("attention" if attention else "") + str(index + 1),
    )(*(array for array, _ in ins.values()))
    return Bag(**dict(zip(outs, result, strict=True)))


def settle_kernel(counts, place, *refs):
    refs = list(refs)
    held = [[refs.pop(0) for _ in range(count)] for count in counts]
    out_a, out_b, zeros, sems = refs
    home = place.shape[1]
    zeros[...] = jnp.zeros_like(zeros)

    def start(s, carry):
        for j, out in enumerate((out_a, out_b)):
            source = place[j, s]

            @pl.when(source < 0)
            def _(out=out, j=j):
                pltpu.make_async_copy(zeros, out.at[s], sems.at[j, s]).start()

            low = 0
            for ref in held[j]:
                high = low + ref.shape[0]

                @pl.when((source >= low) & (source < high))
                def _(ref=ref, out=out, j=j, at=source - low):
                    pltpu.make_async_copy(ref.at[at], out.at[s], sems.at[j, s]).start()

                low = high

        return carry

    lax.fori_loop(0, home, start, 0)

    def finish(s, carry):
        for j, out in enumerate((out_a, out_b)):
            pltpu.make_async_copy(zeros, out.at[s], sems.at[j, s]).wait()
        return carry

    lax.fori_loop(0, home, finish, 0)


def settle(place, first, second):
    home = place.shape[1]
    half_shape = first[0].shape[1:]
    hbm = pl.BlockSpec(memory_space=pl.ANY)
    vmem = pl.BlockSpec(memory_space=pltpu.VMEM)
    shape = jax.ShapeDtypeStruct((home,) + half_shape, BF16)
    counts = (len(first), len(second))
    return pl.pallas_call(
        functools.partial(settle_kernel, counts),
        out_shape=(shape, shape),
        in_specs=[pl.BlockSpec(memory_space=pltpu.SMEM)] + [vmem] * sum(counts),
        out_specs=(hbm, hbm),
        scratch_shapes=[pltpu.VMEM(half_shape, BF16), pltpu.SemaphoreType.DMA((2, home))],
        compiler_params=pltpu.CompilerParams(vmem_limit_bytes=VMEM_LIMIT),
        name="settle",
    )(place, *first, *second)


def local_kernel(jobs, digits_ref, *refs):
    refs = list(refs)
    ins = [[refs.pop(0) for _ in range(count)] for _, count, _, _ in jobs]
    outs = [[refs.pop(0) for _ in range(size if scatter else 1)] for scatter, _, size, _ in jobs]
    assert not refs
    for (scatter, _, size, stage), parts, made in zip(jobs, ins, outs):
        digit = digits_ref[stage]
        if scatter:
            rows = made[0].shape[0]
            for k, out in enumerate(made):
                at = pl.multiple_of((digit ^ k) * rows, rows) if size > 1 else 0
                total = parts[0][pl.ds(at, rows), :].astype(F32)
                for part in parts[1:]:
                    total = total + part[pl.ds(at, rows), :].astype(F32)
                out[...] = total.astype(BF16)
        else:
            rows = parts[0].shape[0]
            for k, part in enumerate(parts):
                made[0][pl.ds(pl.multiple_of((digit ^ k) * rows, rows), rows), :] = part[...]


def dp_groups(devices):
    sizes = []
    while devices > 1:
        size = 4 if devices % 4 == 0 else 2
        sizes.append(size)
        devices //= size
    return sizes


def with_peer(value, stride, k):
    devices = lax.axis_size(DP)
    return lax.ppermute(value, DP, [(d, d ^ (k * stride)) for d in range(devices)])


def stack_kernel(*refs):
    out, pairs = refs[-1], refs[:-1]
    at = 0
    for one, other in zip(pairs[0::2], pairs[1::2]):
        rows = one.shape[0]
        out[at : at + rows, :] = (one[...].astype(F32) + other[...].astype(F32)).astype(BF16)
        at += rows


def stack(*pairs):
    vmem = pl.BlockSpec(memory_space=pltpu.VMEM)
    rows = sum(pair[0].shape[0] for pair in pairs)
    return pl.pallas_call(
        stack_kernel,
        out_shape=jax.ShapeDtypeStruct((rows, pairs[0][0].shape[1]), BF16),
        in_specs=[vmem] * (2 * len(pairs)),
        out_specs=vmem,
        compiler_params=pltpu.CompilerParams(vmem_limit_bytes=VMEM_LIMIT),
        name="stack",
    )(*(value for pair in pairs for value in pair))


class DpSum:
    def __init__(self, parts):
        self.parts = parts
        self.phase = 0
        self.stages, stride = [], 1
        for size in dp_groups(lax.axis_size(DP)):
            self.stages.append((size, stride))
            stride *= size

    def job(self):
        count = len(self.stages)
        if self.phase < count:
            return (True, len(self.parts), self.stages[self.phase][0], self.phase)
        if self.phase == count:
            return (True, len(self.parts), 1, 0)
        stage = 2 * count - self.phase
        return (False, len(self.parts), self.stages[stage][0], stage)

    def accept(self, made):
        count = len(self.stages)
        if self.phase < count:
            size, stride = self.stages[self.phase]
            self.parts = [made[0]] + [with_peer(made[k], stride, k) for k in range(1, size)]
        elif self.phase < 2 * count:
            size, stride = self.stages[2 * count - 1 - self.phase]
            self.parts = [made[0]] + [with_peer(made[0], stride, k) for k in range(1, size)]
        else:
            self.parts = made
        self.phase += 1

    def last(self):
        return self.phase >= 2 * len(self.stages)


def advance(sums, digits, *ties):
    sums = [s for s in sums if not s.last()]
    if not sums:
        return ties
    jobs = [s.job() for s in sums]
    inputs, shapes, counts = [], [], []
    for s, (scatter, count, size, _) in zip(sums, jobs):
        rows, width = s.parts[0].shape
        inputs += s.parts
        made = [(rows // size, width)] * size if scatter else [(rows * size, width)]
        shapes += made
        counts.append(len(made))
    smem = pl.BlockSpec(memory_space=pltpu.SMEM)
    vmem = pl.BlockSpec(memory_space=pltpu.VMEM)
    outs = pl.pallas_call(
        functools.partial(local_kernel, jobs),
        out_shape=tuple(jax.ShapeDtypeStruct(shape, BF16) for shape in shapes),
        in_specs=[smem] + [vmem] * len(inputs),
        out_specs=(vmem,) * len(shapes),
        compiler_params=pltpu.CompilerParams(vmem_limit_bytes=VMEM_LIMIT),
        name="fold",
    )(digits, *inputs)
    outs, ties = lax.optimization_barrier((list(outs), ties))
    for s, count in zip(sums, counts):
        s.accept(outs[:count])
        outs = outs[count:]
    return ties


def unpack_kernel(layout, count, digit_ref, *refs):
    refs = list(refs)
    pieces = [[refs.pop(0) for _ in range(count)] for _ in range(2)]
    whole_two = refs.pop(0)
    up, down, inward, out, earth, hidden, entry, *rest_refs = refs
    small, joined = rest_refs[:6], rest_refs[6:]
    digit = digit_ref[0]
    for parts, whole in zip(pieces, joined):
        rows = parts[0].shape[0]
        for k, piece in enumerate(parts):
            whole[pl.ds(pl.multiple_of((digit ^ k) * rows, rows), rows), :] = piece[...]
    width = up.shape[1]
    hidden_part = up.shape[2]
    part = width // 2
    win = earth.shape[2]
    third = win // 3
    split = joined[0].shape[0]
    packs = [(joined[0], 0, joined[1], 0), (whole_two, 0, whole_two, split)]
    for b, (pack, base, other, base_other) in enumerate(packs):
        for at in range(0, hidden_part, width):
            low = base + at
            up[b, :, at : at + width] = pack[low : low + width, :].astype(F32)
            low += hidden_part
            down[b, at : at + width, :] = pack[low : low + width, :].T.astype(F32)

        def lines_of(place, start, size):
            low = base_other + place + start
            return other[low : low + size, :].astype(F32)

        for j in range(3):
            inward[b, j] = lines_of(layout.inward, j * part, part)
        low = base + 2 * hidden_part
        out[b] = pack[low : low + part, :].astype(F32)
        rest = lines_of(layout.rest, 0, third)
        rest = jnp.concatenate([rest[:, k * 128 : (k + 1) * 128] for k in range(3)], axis=0)
        for k in range(earth.shape[1]):
            main = lines_of(layout.earth, (k // 3) * win, win)
            earth[b, k, :, :128] = main[:, (k % 3) * 128 : (k % 3 + 1) * 128]
            earth[b, k, :, 128:] = rest[:, k * (win - 128) : (k + 1) * (win - 128)]
        lines = lines_of(layout.small, 0, 16)
        for k, table in enumerate(small):
            table[b : b + 1, :] = lines[k : k + 1]
        for j, at in enumerate(range(0, hidden_part, width)):
            hidden[b : b + 1, at : at + width] = lines[6 + j : 7 + j]
        last = lines[6 + hidden_part // width : 7 + hidden_part // width]
        entry[b, 0:1] = last[:, :part]
        entry[b, 1:2] = last[:, part:]


def unpack(digit, hidden_parts, attention_parts, whole_two, width, hidden_part, own_heads, win):
    vmem = pl.BlockSpec(memory_space=pltpu.VMEM)
    shapes = (
        (2, width, hidden_part),
        (2, hidden_part, width),
        (2, 3, width // 2, width),
        (2, width // 2, width),
        (2, own_heads, win, win),
        (2, hidden_part),
        (2, 2, width // 2),
    ) + ((2, width),) * 6
    count = len(hidden_parts)
    return pl.pallas_call(
        functools.partial(unpack_kernel, pack_rows(width, own_heads, win), count),
        out_shape=tuple(jax.ShapeDtypeStruct(shape, F32) for shape in shapes),
        in_specs=[pl.BlockSpec(memory_space=pltpu.SMEM)] + [vmem] * (2 * count + 1),
        out_specs=(vmem,) * len(shapes),
        scratch_shapes=[
            pltpu.VMEM((parts[0].shape[0] * count, width), BF16) for parts in (hidden_parts, attention_parts)
        ],
        compiler_params=pltpu.CompilerParams(vmem_limit_bytes=VMEM_LIMIT),
        name="unpack",
    )(digit, *hidden_parts, *attention_parts, whole_two)


def across(value):
    return lax.ppermute(value, TENSOR, [(0, 1), (1, 0)])


def local(
    tokens,
    token_mask,
    shift_next,
    cotangent,
    attend_gain,
    attend_shift,
    inward_weight,
    inward_bias,
    earth_bias,
    outward_weight,
    outward_bias,
    mixer_gain,
    mixer_shift,
    up_weight,
    up_bias,
    down_weight,
    down_bias,
):
    home, half, width = tokens.shape
    cap = home // 2
    part = lax.axis_index(TENSOR).astype(I32).reshape(1)
    tokens_oth = across(tokens)
    inward = jnp.transpose(inward_weight, (0, 2, 3, 1))
    own_heads = earth_bias.shape[1]
    hidden_part = up_weight.shape[2]
    win = 2 * half
    cotangent_oth = across(cotangent)
    meta, tab, place = make_plan(part, token_mask, shift_next, cap)
    common = dict(
        meta=meta,
        tab=tab,
        gain_one=attend_gain,
        shift_one=attend_shift,
        out_bias=outward_bias,
        gain_two=mixer_gain,
        shift_two=mixer_shift,
        down_bias=down_bias,
        entry_own=inward_bias,
        entry_oth=across(inward_bias),
        up_bias_own=up_bias,
        up_bias_oth=across(up_bias),
        in_own=inward,
        in_oth=across(inward),
        earth_own=earth_bias,
        earth_oth=across(earth_bias),
        out_own=outward_weight,
        out_oth=across(outward_weight),
        up_own=up_weight,
        up_oth=across(up_weight),
        down_own=down_weight,
        down_oth=across(down_weight),
    )
    sizes = (cap, half, width, own_heads, hidden_part)
    devices = lax.axis_size(DP)

    def run(stages, index, *more, split=(0, 1)):
        given = dict(common)
        for group in more:
            given.update(vars(group))
        return run_block(stages, index, Bag(**given), sizes, devices, split)

    rank = lax.axis_index(DP).astype(I32)
    digits, stride = [], 1
    for size in dp_groups(devices):
        digits.append(rank // stride % size)
        stride *= size
    digits = jnp.stack(digits)

    def sum_of(kernel):
        return DpSum([kernel.pack_own, across(kernel.pack_oth)])

    first = Bag(src=tokens, src_oth=tokens_oth)
    ahead_one = run((True, False, False), 0, first)
    second = Bag(src=ahead_one.out, src_oth=across(ahead_one.out_half))
    mixer_two = run((True, True, False), 1, second, Bag(grad_src=cotangent, grad_oth=cotangent_oth))
    pack_far = across(mixer_two.pack_oth)
    recv_b = across(mixer_two.send)
    attention_two = run((False, False, True), 1, mixer_two, second)
    half_far = across(attention_two.out_half)
    pack_two = stack((mixer_two.pack_own, pack_far), (attention_two.pack_own, across(attention_two.pack_oth)))
    pack_two, half_far = lax.optimization_barrier((pack_two, half_far))
    sum_two = lax.psum(pack_two, DP)
    back = Bag(grad_src=attention_two.out, grad_oth=half_far)
    mixer_one = run((False, True, False), 0, ahead_one, first, back)
    sum_mixer_one = sum_of(mixer_one)
    (do,) = advance([sum_mixer_one], digits, mixer_one.do)
    halves, across_one = [], []
    for which in range(PARTS):
        if which:
            (do,) = advance([sum_mixer_one], digits, do)
        halves.append(run((False, False, True), 0, ahead_one, mixer_one, Bag(do=do), first, split=(which, PARTS)))
        far, parts = lax.optimization_barrier((halves[-1].pack_oth, sum_mixer_one.parts))
        sum_mixer_one.parts = parts
        across_one.append(across(far))
    sum_attention_one = DpSum([half_of.pack_own for half_of in halves] + across_one)
    recv_a = [across(half_of.send) for half_of in halves]
    sums = [sum_mixer_one, sum_attention_one]
    while not all(s.last() for s in sums):
        advance(sums, digits)
    tokens_grad, block_output = settle(
        place, [half_of.keep for half_of in halves] + recv_a, [mixer_two.keep, recv_b]
    )
    g_up, g_down, g_in, g_out, g_earth, hidden, entry, *small = unpack(
        digits[:1], sum_mixer_one.parts, sum_attention_one.parts, sum_two, width, hidden_part, own_heads, win
    )
    return (
        block_output,
        tokens_grad,
        small[0],
        small[1],
        jnp.transpose(g_in, (0, 3, 1, 2)),
        entry,
        g_earth,
        g_out,
        small[2],
        small[3],
        small[4],
        g_up,
        hidden,
        g_down,
        small[5],
    )


def solution(mesh):
    placed = (
        P(DP, TENSOR, None),
        P(DP, None),
        P(DP),
        P(DP, TENSOR, None),
        P(),
        P(),
        P(None, None, None, TENSOR),
        P(None, None, TENSOR),
        P(None, TENSOR, None, None),
        P(None, TENSOR, None),
        P(),
        P(),
        P(),
        P(None, None, TENSOR),
        P(None, TENSOR),
        P(None, TENSOR, None),
        P(),
    )
    return jax.shard_map(
        local,
        mesh=mesh,
        in_specs=placed,
        out_specs=(
            P(DP, TENSOR, None),
            P(DP, TENSOR, None),
            P(),
            P(),
            P(None, None, None, TENSOR),
            P(None, None, TENSOR),
            P(None, TENSOR, None, None),
            P(None, TENSOR, None),
            P(),
            P(),
            P(),
            P(None, None, TENSOR),
            P(None, TENSOR),
            P(None, TENSOR, None),
            P(),
        ),
        check_vma=False,
    )
```

```python
import functools
from types import SimpleNamespace as Bag

import jax
import jax.numpy as jnp
from jax import lax
from jax.experimental import pallas as pl
from jax.experimental.pallas import tpu as pltpu
from jax.sharding import PartitionSpec as P

F32 = jnp.float32
BF16 = jnp.bfloat16
I32 = jnp.int32

CHUNK = 4
TILE = 4
DP = "dp"
TENSOR = "tensor"
LATS = 6
HALF_COLS = 6
COST_CUT = 64
PARTS = 1
LN2 = 0.6931471805599453
NEVER = -1000000000.0
VMEM_LIMIT = 60 * 1024 * 1024


def mm(a, b):
    return lax.dot_general(a, b, (((1,), (0,)), ((), ())), preferred_element_type=F32)


def mm_nt(a, b):
    return lax.dot_general(a, b, (((1,), (1,)), ((), ())), preferred_element_type=F32)


def mm_tn(a, b):
    return lax.dot_general(a, b, (((0,), (0,)), ((), ())), preferred_element_type=F32)


def fold_rows(values):
    rows, width = values.shape
    return jnp.sum(values.reshape(rows // 8, 8, width), axis=0)


def plan_kernel(t_ref, mask_ref, next_ref, meta_ref, tab_ref, place_ref, seen, order, first, last, rows, cols):
    home = next_ref.shape[0]
    cap = tab_ref.shape[1]
    half = mask_ref.shape[1] // 2
    t = t_ref[0]

    def clear(s, carry):
        seen[s] = 0
        place_ref[0, s] = -1
        place_ref[1, s] = -1
        high = mask_ref[s, 0]
        for i in range(1, LATS):
            high += mask_ref[s, i * HALF_COLS]
        wide = mask_ref[s, 0] + mask_ref[s, half]
        for j in range(1, HALF_COLS):
            wide += mask_ref[s, j] + mask_ref[s, half + j]
        rows[s] = high
        cols[s] = wide
        return carry

    lax.fori_loop(0, home, clear, 0)

    def visit(origin, count):
        fresh = (rows[origin] > 0) & (seen[origin] == 0)

        def walk(carry):
            s, at, _ = carry
            seen[s] = 1
            order[at] = s
            first[at] = count
            following = next_ref[s]
            return following, at + 1, (following != origin) & (at + 1 < home)

        return lax.while_loop(lambda carry: carry[2], walk, (origin, count, fresh))[1]

    total = lax.fori_loop(0, home, visit, 0)

    def close(back, carry):
        p = total - 1 - back
        after = jnp.minimum(p + 1, home - 1)
        ends = (p == total - 1) | (first[after] != first[p])
        end = jnp.where(ends, p, carry)
        last[p] = end
        return end

    lax.fori_loop(0, total, close, 0)

    cut = (total + 1) // 2
    base = t * cut
    n = jnp.where(t == 0, cut, total - cut)

    def fill(i, carry):
        live = i < n
        p = jnp.where(live, base + i, 0)
        slot = jnp.where(live, order[p], 0)
        ahead = jnp.where(p == last[p], first[p], p + 1)
        behind = jnp.where(p == first[p], last[p], p - 1)
        next_slot = next_ref[slot]
        ahead_in = live & (ahead >= base) & (ahead < base + n)
        behind_in = live & (behind >= base) & (behind < base + n)
        tab_ref[0, i] = slot
        tab_ref[1, i] = jnp.where(ahead_in, ahead - base, -1)
        tab_ref[2, i] = jnp.where(behind_in, behind - base, -1)
        tab_ref[3, i] = jnp.where(live, rows[slot], 0)
        tab_ref[4, i] = jnp.where(live, cols[slot], 0)
        tab_ref[5, i] = jnp.where(live, rows[next_slot], 0)
        tab_ref[6, i] = jnp.where(live, cols[next_slot], 0)
        tab_ref[7, i] = jnp.where(live, next_slot, 0)
        return carry

    @pl.when(total == 0)
    def _():
        order[0] = 0
        first[0] = 0
        last[0] = 0

    lax.fori_loop(0, cap, fill, 0)

    def settle(p, carry):
        slot = order[p]
        owner = jnp.where(p >= cut, 1, 0)
        here = p - owner * cut
        source = jnp.where(owner == t, here, cap + here)
        place_ref[0, slot] = source
        place_ref[1, jnp.where(t == 1, slot, next_ref[slot])] = source
        return carry

    lax.fori_loop(0, total, settle, 0)

    crossing = (cut < total) & (first[jnp.minimum(cut, home - 1)] < cut)
    tail = jnp.maximum(cut - 1, 0)
    meta_ref[0] = n
    meta_ref[1] = jnp.where(crossing & (t == 0), first[jnp.minimum(cut, home - 1)], 0)
    meta_ref[2] = jnp.where(t == 0, tail, jnp.where(crossing, last[tail] - cut, 0))
    meta_ref[3] = t
    for spare in range(4, 8):
        meta_ref[spare] = 0


def make_plan(part, token_mask, shift_next, cap):
    home = shift_next.shape[0]
    smem = pl.BlockSpec(memory_space=pltpu.SMEM)
    return pl.pallas_call(
        plan_kernel,
        out_shape=(
            jax.ShapeDtypeStruct((8,), I32),
            jax.ShapeDtypeStruct((8, cap), I32),
            jax.ShapeDtypeStruct((2, home), I32),
        ),
        in_specs=[smem, smem, smem],
        out_specs=(smem, smem, smem),
        scratch_shapes=[pltpu.SMEM((home,), I32) for _ in range(6)],
        cost_estimate=pl.CostEstimate(flops=5 * 10**9, bytes_accessed=2**24, transcendentals=0),
        name="plan",
    )(part, token_mask, shift_next)


def gelu_pair(u):
    cdf = 0.5 + 0.5 * lax.erf(u * 0.7071067811865476)
    return u * cdf, cdf + u * (0.3989422804014327 * jnp.exp(-0.5 * (u * u)))


def normalise(values):
    centred = values - jnp.mean(values, axis=-1, keepdims=True)
    spread = jnp.mean(centred * centred, axis=-1, keepdims=True)
    scale = lax.rsqrt(spread + 1e-05)
    return centred * scale, scale


def norm_back(grad, unit, scale, gain):
    inner = grad * gain
    mean_one = jnp.mean(inner, axis=-1, keepdims=True)
    mean_two = jnp.mean(inner * unit, axis=-1, keepdims=True)
    return scale * (inner - mean_one - unit * mean_two)


def block_kernel(names, stages, index, head_width, span_of, *refs):
    ref = Bag(**dict(zip(names, refs, strict=True)))
    ahead, mixer, attention = stages
    if ahead or attention:
        in_sides = (ref.in_own, ref.in_oth)
    if ahead or mixer:
        out_sides, up_sides, down_sides = ((ref.out_own, ref.out_oth), (ref.up_own, ref.up_oth), (ref.down_own, ref.down_oth))
    if ahead:
        earth_sides, entry_sides = (ref.earth_own, ref.earth_oth), (ref.entry_own, ref.entry_oth)
        up_bias_sides = (ref.up_bias_own, ref.up_bias_oth)
    if mixer or attention:
        pack_sides = (ref.pack_own, ref.pack_oth)
    shifted = index == 1
    meta, tab = ref.meta, ref.tab
    cap = tab.shape[1]
    half, width = ref.xs.shape[2:]
    win = 2 * half
    rows_all = CHUNK * win
    part = width // 2
    groups = width // 128
    per_group = 128 // head_width
    heads = width // head_width
    own_heads = heads // 2
    scale = head_width**-0.5
    n = meta[0]
    t = meta[3]
    lead, span_count = span_of
    step = pl.program_id(0)
    w0 = lead + step * CHUNK
    first_step = step == 0
    lanes = lax.broadcasted_iota(I32, (1, 128), 1) // head_width
    head_keep = [jnp.where(lanes == k, 1.0, 0.0).astype(BF16) for k in range(per_group)]
    lane = lax.broadcasted_iota(I32, (win, 128), 1)
    spots = [((u + 1) % per_group) * head_width for u in range(per_group)]
    spare_lane = [lane == spot for spot in spots]
    spare_two = [(lane == spot) | (lane == spot + 1) for spot in spots]
    one = jnp.ones((), BF16)
    pitch = -(-win // 256) * 256
    blank_lanes = jnp.zeros((win, pitch - win), BF16)
    blank_rows = jnp.zeros((pitch - win, 128), BF16)
    wide_step = TILE * win

    def row(table):
        return table[index : index + 1, :]

    def by_part(west, one_ref, other, at, dst, sem):
        is_own = t == (0 if west else 1)

        @pl.when(is_own)
        def _():
            pltpu.make_async_copy(one_ref.at[at], dst, sem).start()

        @pl.when(jnp.logical_not(is_own))
        def _():
            pltpu.make_async_copy(other.at[at], dst, sem).start()

    def by_place(local, local_half, one_ref, other, dst, sem):
        @pl.when(local >= 0)
        def _():
            pltpu.make_async_copy(one_ref.at[local, local_half], dst, sem).start()

        @pl.when(local < 0)
        def _():
            pltpu.make_async_copy(other, dst, sem).start()

    xs, x_sem = ref.xs, ref.x_sem
    if mixer:
        rs, r_sem = ref.rs, ref.r_sem

    if ahead:
        bias_copies = [
            pltpu.make_async_copy(
                side.at[index], ref.bias.at[pl.ds(s * own_heads, own_heads)], ref.b_sem.at[s]
            )
            for s, side in enumerate(earth_sides)
        ]

    @pl.when(first_step)
    def _():
        if ahead:
            for copy in bias_copies:
                copy.start()

        def start_loads(i, carry):
            if shifted:
                by_place(i, 1, ref.src, ref.src_oth, xs.at[i, 0], x_sem.at[i, 0])
                by_place(tab[1, i], 0, ref.src, ref.src_oth, xs.at[i, 1], x_sem.at[i, 1])
            else:
                by_part(True, ref.src, ref.src_oth, tab[0, i], xs.at[i, 0], x_sem.at[i, 0])
                by_part(False, ref.src, ref.src_oth, tab[0, i], xs.at[i, 1], x_sem.at[i, 1])
            if mixer and shifted:
                by_part(False, ref.grad_src, ref.grad_oth, tab[0, i], rs.at[i, 0], r_sem.at[i, 0])
                by_part(True, ref.grad_src, ref.grad_oth, tab[7, i], rs.at[i, 1], r_sem.at[i, 1])
            elif mixer:
                by_place(tab[2, i], 1, ref.grad_src, ref.grad_oth, rs.at[i, 0], r_sem.at[i, 0])
                by_place(i, 0, ref.grad_src, ref.grad_oth, rs.at[i, 1], r_sem.at[i, 1])
            return carry

        lax.fori_loop(lead, jnp.minimum(lead + span_count, n), start_loads, 0)

        def blank(i, carry):
            for k in range(2):
                xs[i, k] = jnp.zeros_like(xs[i, k])
                if mixer:
                    rs[i, k] = jnp.zeros_like(rs[i, k])
            return carry

        lax.fori_loop(jnp.maximum(n, lead), lead + span_count, blank, 0)
        if mixer:
            from_head = lax.broadcasted_iota(I32, (width, width), 0) // head_width
            to_head = lax.broadcasted_iota(I32, (width, width), 1) // head_width
            same = from_head // per_group == to_head // per_group
            following = (from_head + 1) % per_group == to_head % per_group
            ref.spread[...] = jnp.where(same & following, 1.0, 0.0).astype(BF16)
        if ahead or attention:
            for j in range(3):
                for s, side in enumerate(in_sides):
                    at = j * width + s * part
                    ref.w_in[at : at + part, :] = side[j]
        if ahead or mixer:
            for s, side in enumerate(out_sides):
                ref.wo[s * part : (s + 1) * part, :] = side[...]
            level = LATS * HALF_COLS
            place = lax.broadcasted_iota(I32, (win, 128), 0)
            inside = place
            for bound in (level, 2 * level, 3 * level):
                inside = inside - jnp.where(place >= bound, level, 0)
            lat = jnp.zeros_like(inside)
            for bound in range(HALF_COLS, level, HALF_COLS):
                lat = lat + jnp.where(inside >= bound, 1, 0)
            ref.lat[...] = lat
            ref.col[...] = inside - HALF_COLS * lat
        if ahead:
            for copy in bias_copies:
                copy.wait()
            for k in range(heads):
                ref.bias[k] = ref.bias[k] * (1.0 / LN2)
        sums = [ref.acc_small] if mixer or attention else []
        if mixer:
            sums += [ref.acc_up, ref.acc_down, ref.acc_out, ref.acc_hidden]
        if attention:
            sums += [ref.acc_in, ref.acc_earth, ref.acc_entry]
        for table in sums:
            table[...] = jnp.zeros_like(table)

    def extents(i):
        high, wide, high_next, wide_next = tab[3, i], tab[4, i], tab[5, i], tab[6, i]
        if shifted:
            return (high, wide - HALF_COLS), (high_next, wide_next)
        return (high, wide), (high, wide - HALF_COLS)

    def valid_rows(i, k):
        high, wide = extents(i)[k]
        valid = (ref.lat[:half] < high) & (ref.col[:half] < wide)
        return jnp.concatenate([jnp.where(valid, 1.0, 0.0)] * groups, axis=1)

    def tile_x(tile):
        parts = []
        for j in range(TILE):
            for k in range(2):
                parts.append(xs[w0 + tile * TILE + j, k].astype(F32))
        return jnp.concatenate(parts, axis=0)

    def entrance(tile, c):
        rows = pl.ds(pl.multiple_of(tile * wide_step, wide_step), wide_step)
        unit, _ = normalise(tile_x(tile))
        low = (unit * row(ref.gain_one) + row(ref.shift_one)).astype(BF16)
        ref.h1[rows, :] = low
        for j in range(3):
            cols = slice(j * width, (j + 1) * width)
            value = mm_nt(low, ref.w_in[cols, :])
            if j != 1:
                value = value + jnp.concatenate(
                    [side[index, j // 2 : j // 2 + 1, :] for side in entry_sides], axis=1
                )
            if j == 0:
                value = value * (scale / LN2)
            ref.qkv[rows, cols] = value.astype(BF16)
        return c

    def attend(pair, c):
        for j in range(2):
            attend_one(pair * 2 + j)
        return c

    def attend_one(w):
        rows = pl.ds(pl.multiple_of(w * win, win), win)
        (high_a, wide_a), (high_b, wide_b) = extents(w0 + w)
        west = lax.broadcasted_iota(I32, (win, 128), 0) < half
        high = jnp.where(west, high_a, high_b)
        wide = jnp.where(west, wide_a, wide_b)
        hide = jnp.where((ref.lat[...] < high) & (ref.col[...] < wide), 0.0, NEVER).astype(BF16)
        for g in range(groups):
            span = [slice(j * width + g * 128, j * width + (g + 1) * 128) for j in range(3)]
            q, k, v = (ref.qkv[rows, cols] for cols in span)
            total = []
            for u in range(per_group):
                head = g * per_group + u
                spare = spare_lane[u]
                s = mm_nt(jnp.where(spare, one, q * head_keep[u]), jnp.where(spare, hide, k))
                s = s + ref.bias[head]
                low = jnp.exp2(s - jnp.max(s, axis=-1, keepdims=True)).astype(BF16)
                ref.probs[w, head] = low
                total.append(jnp.concatenate([low, blank_lanes], axis=1))
            tall = [value for keep in head_keep for value in (v * keep, blank_rows)]
            ones = [value for keep in head_keep for value in (jnp.broadcast_to(keep, (win, 128)), blank_rows)]
            tall = jnp.concatenate([jnp.concatenate(tall, axis=0), jnp.concatenate(ones, axis=0)], axis=1)
            total = mm(jnp.concatenate(total, axis=1), tall)
            inverse = 1.0 / total[:, 128:]
            cols = slice(g * 128, (g + 1) * 128)
            ref.att[rows, cols] = (total[:, :128] * inverse).astype(BF16)
            ref.inverse[rows, cols] = inverse.astype(BF16)

    hidden_part = up_sides[0].shape[1] if ahead or mixer else 0
    hidden = 2 * hidden_part
    pieces = [(s, at) for s in range(2) for at in range(0, hidden_part, 384)]

    def middle(tile, c):
        rows = pl.ds(pl.multiple_of(tile * wide_step, wide_step), wide_step)
        att = ref.att[rows, :]
        v2 = tile_x(tile) + mm(att, ref.wo[...]) + row(ref.out_bias)
        unit, unit_scale = normalise(v2)
        if ahead:
            low = (unit * row(ref.gain_two) + row(ref.shift_two)).astype(BF16)
            ref.h2[rows, :] = low
            result = v2 + row(ref.down_bias)
        if mixer:
            parts = []
            for j in range(TILE):
                i = w0 + tile * TILE + j
                for k in range(2):
                    r = rs[i, k].astype(F32)
                    if shifted:
                        r = r * valid_rows(i, k)
                    parts.append(r)
            r = jnp.concatenate(parts, axis=0)
            r_low = r.astype(BF16)
            ref.rr[rows, :] = r_low
        for s, off in pieces:
            cols = slice(off, off + 384)
            at = off + s * hidden_part
            span = slice(at, at + 384)
            if ahead:
                u = mm(low, up_sides[s][:, cols]) + up_bias_sides[s][index : index + 1, cols]
                g, slope = gelu_pair(u)
                g = g.astype(BF16)
                ref.act[rows, span] = g
                if not mixer:
                    ref.slope[rows, span] = slope.astype(BF16)
            else:
                slope = ref.slope[rows, span].astype(F32)
            if mixer:
                du = mm_nt(r_low, down_sides[s][cols, :]) * slope
                ref.acc_hidden[:, span] += fold_rows(du)
                du = du.astype(BF16)
                ref.du[rows, span] = du
        sides = [slice(s * hidden_part, (s + 1) * hidden_part) for s in range(2)]
        if ahead:
            for side, cols in zip(down_sides, sides):
                result = result + mm(ref.act[rows, cols], side[...])
        if mixer:
            d_h2 = mm_nt(ref.du[rows, sides[0]], up_sides[0][...]) + mm_nt(ref.du[rows, sides[1]], up_sides[1][...])
        if ahead:
            for j in range(TILE):
                i = w0 + tile * TILE + j
                for k in range(2):
                    at = j * win + k * half
                    piece = result[at : at + half]
                    if not shifted:
                        ref.out[i, k] = piece.astype(BF16)
                        continue
                    piece = (piece * valid_rows(i, k)).astype(BF16)
                    place_half(ref.keep, ref.send, i, 1 - k, piece)
        if mixer:
            ref.acc_small[5] += fold_rows(r)
            ref.acc_small[4] += fold_rows(d_h2)
            ref.acc_small[3] += fold_rows(d_h2 * unit)
            dv2 = r + norm_back(d_h2, unit, unit_scale, row(ref.gain_two))
            ref.acc_small[2] += fold_rows(dv2)
            da = dv2.astype(BF16)
            ref.da[rows, :] = da
            d_att = mm_nt(da, ref.wo[...]) * ref.inverse[rows, :].astype(F32)
            ref.do[rows, :] = d_att.astype(BF16)
            inner = (d_att * att.astype(F32)).astype(BF16)
            delta = -mm(inner, ref.spread[...])
            high = delta.astype(BF16)
            rest = (delta - high.astype(F32)).astype(BF16)
            spot = lax.broadcasted_iota(I32, (1, width), 1) % head_width
            ref.aug[rows, :] = jnp.where(spot == 0, high, jnp.where(spot == 1, rest, jnp.zeros_like(rest)))
        return c

    def place_half(keep, send, i, owner, piece):
        @pl.when(t == owner)
        def _():
            keep[i] = piece

        @pl.when(t != owner)
        def _():
            send[i] = piece

    def hidden_grads(_, c):
        r_turned = ref.rr[...].T
        h_turned = ref.h2[...].T
        for at in range(0, hidden, 256):
            cols = slice(at, at + 256)
            ref.acc_down[:, cols] += mm(r_turned, ref.act[:, cols])
            ref.acc_up[:, cols] += mm(h_turned, ref.du[:, cols])
        ref.acc_out[...] += mm(ref.att[...].T, ref.da[...])
        return c

    def attend_back(pair, c):
        spans = [pl.ds(pl.multiple_of((pair * 2 + j) * win, win), win) for j in range(2)]
        for g in range(groups):
            span = [slice(j * width + g * 128, j * width + (g + 1) * 128) for j in range(3)]
            here = slice(g * 128, (g + 1) * 128)
            loaded = []
            for rows in spans:
                q, k, v = (ref.qkv[rows, cols] for cols in span)
                dog = ref.do[rows, here]
                loaded.append((q.T, k, v, dog, dog.T, ref.aug[rows, here], [], [], []))
            for u in range(per_group):
                head = g * per_group + u
                cut = slice(u * head_width, (u + 1) * head_width)
                total = None
                for j in range(2):
                    q_turned, k, v, dog, do_turned, augment, dq, dk, dv = loaded[j]
                    low = ref.probs[pair * 2 + j, head]
                    dom = jnp.where(spare_two[u], augment, dog * head_keep[u])
                    dp = mm_nt(dom, jnp.where(spare_two[u], one, v))
                    ds = low.astype(F32) * dp
                    total = ds if total is None else total + ds
                    ds = ds.astype(BF16)
                    dk.append(mm(q_turned[cut], ds))
                    dv.append(mm(do_turned[cut], low))
                    dq.append(jnp.concatenate([ds, blank_lanes], axis=1))
                ref.acc_earth[head] += total
            for j, rows in enumerate(spans):
                dq, dk, dv = loaded[j][6:]
                k = loaded[j][1]
                tall = [value for keep in head_keep for value in (k * keep, blank_rows)]
                dq = mm(jnp.concatenate(dq, axis=1), jnp.concatenate(tall, axis=0)) * scale
                dk = (jnp.concatenate(dk, axis=0) * LN2).T
                dv = jnp.concatenate(dv, axis=0).T
                for at, value in ((0, dq), (2, dv)):
                    ref.acc_entry[:, span[at]] += fold_rows(value)
                for at, value in enumerate((dq, dk, dv)):
                    ref.dqkv[rows, span[at]] = value.astype(BF16)
        return c

    def exit_back(tile, c):
        rows = pl.ds(pl.multiple_of(tile * wide_step, wide_step), wide_step)
        unit, unit_scale = normalise(tile_x(tile))
        dh = mm(ref.dqkv[rows, :], ref.w_in[...])
        ref.acc_small[1] += fold_rows(dh)
        ref.acc_small[0] += fold_rows(dh * unit)
        dv = ref.da[rows, :].astype(F32) + norm_back(dh, unit, unit_scale, row(ref.gain_one))
        for j in range(TILE):
            i = w0 + tile * TILE + j
            for k in range(2):
                at = j * win + k * half
                piece = dv[at : at + half].astype(BF16)
                if shifted:
                    ref.out[i, k] = piece
                else:
                    place_half(ref.keep, ref.send, i - lead, k, piece)
        return c

    def weight_grads(_, c):
        turned = ref.h1[...].T
        for j in range(3):
            cols = slice(j * width, (j + 1) * width)
            ref.acc_in[:, cols] += mm(turned, ref.dqkv[:, cols])
        return c

    @pl.when(w0 < n)
    def _():
        def wait_loads(i, c):
            for k in range(2):
                pltpu.make_async_copy(xs.at[i, k], xs.at[i, k], x_sem.at[i, k]).wait()
                if mixer:
                    pltpu.make_async_copy(rs.at[i, k], rs.at[i, k], r_sem.at[i, k]).wait()
            return c

        lax.fori_loop(w0, jnp.minimum(w0 + CHUNK, n), wait_loads, 0)
        if ahead:
            lax.fori_loop(0, CHUNK // TILE, entrance, 0)
            lax.fori_loop(0, CHUNK // 2, attend, 0)
        if ahead or mixer:
            lax.fori_loop(0, CHUNK // TILE, middle, 0)
        if mixer:
            lax.fori_loop(0, 1, hidden_grads, 0)
        if attention:
            lax.fori_loop(0, CHUNK // 2, attend_back, 0)
            lax.fori_loop(0, CHUNK // TILE, exit_back, 0)
            lax.fori_loop(0, 1, weight_grads, 0)

    @pl.when(step == pl.num_programs(0) - 1)
    def _():
        if ahead and not shifted:
            ref.out_half[...] = ref.out[meta[1], 0]
        if attention and shifted:
            ref.out_half[...] = ref.out[meta[2], 1]
        if mixer:
            for s, pack in enumerate(pack_sides):
                base = s * hidden_part
                for at in range(0, hidden_part, width):
                    cols = slice(base + at, base + at + width)
                    pack[at : at + width, :] = ref.acc_up[:, cols].astype(BF16)
                    pack[hidden_part + at : hidden_part + at + width, :] = ref.acc_down[:, cols].astype(BF16)
                low, high = 2 * hidden_part, 2 * hidden_part + part
                pack[low:high, :] = ref.acc_out[s * part : (s + 1) * part, :].astype(BF16)
                if pack.shape[0] > high:
                    pack[high:, :] = jnp.zeros_like(pack[high:, :])
            ref.sums_small[...] = jnp.sum(ref.acc_small[...], axis=1)
            ref.sums_hidden[...] = jnp.sum(ref.acc_hidden[...], axis=0, keepdims=True)
        if attention:
            small = jnp.sum(ref.acc_small[...], axis=1)
            hidden_sum = ref.sums_hidden[...]
            if lead == 0:
                small = small + ref.sums_small[...]
            else:
                hidden_sum = jnp.zeros_like(hidden_sum)
            half_hidden = hidden_sum.shape[1] // 2
            entry_sum = jnp.sum(ref.acc_entry[...], axis=0, keepdims=True)
            layout = pack_rows(width, own_heads, win)
            for s, pack in enumerate(pack_sides):
                cuts = [slice(j * width + s * part, j * width + (s + 1) * part) for j in range(3)]
                for j, cut in enumerate(cuts):
                    at = layout.inward + j * part
                    pack[at : at + part, :] = ref.acc_in[:, cut].T.astype(BF16)
                earth = [ref.acc_earth[s * own_heads + k] for k in range(own_heads)]
                for k, value in enumerate(earth):
                    row_at = layout.earth + (k // 3) * win
                    pack[row_at : row_at + win, (k % 3) * 128 : (k % 3 + 1) * 128] = value[:, :128].astype(BF16)
                rest = jnp.concatenate([value[:, 128:] for value in earth], axis=1)
                rest = jnp.concatenate([rest, jnp.zeros((win, 128 - rest.shape[1]), F32)], axis=1)
                third = win // 3
                for k in range(3):
                    pack[layout.rest : layout.rest + third, k * 128 : (k + 1) * 128] = rest[
                        k * third : (k + 1) * third
                    ].astype(BF16)
                lines = [small]
                for at in range(s * half_hidden, (s + 1) * half_hidden, width):
                    lines.append(hidden_sum[:, at : at + width])
                lines.append(jnp.concatenate([entry_sum[:, cuts[0]], entry_sum[:, cuts[2]]], axis=1))
                count = small.shape[0] + len(lines) - 1
                lines.append(jnp.zeros((16 - count, width), F32))
                pack[layout.small : layout.small + 16, :] = jnp.concatenate(lines, axis=0).astype(BF16)
                if pack.shape[0] > layout.total:
                    pack[layout.total :, :] = jnp.zeros_like(pack[layout.total :, :])


def pack_rows(width, own_heads, win):
    counts = dict(
        inward=3 * width // 2, earth=own_heads // 3 * win, rest=win // 3, small=16, total=0
    )
    layout, at = {}, 0
    for name, count in counts.items():
        layout[name] = at
        at += count
    return Bag(**layout)


def padded(rows, devices):
    unit = 16 * devices
    return -(-rows // unit) * unit


def run_block(stages, index, given, sizes, devices, split):
    cap, half, width, own_heads, hidden_part = sizes
    ahead, mixer, attention = stages
    shifted = index == 1
    win = 2 * half
    rows = CHUNK * win
    heads = 2 * own_heads
    hidden = 2 * hidden_part
    head_width = width // heads
    which, parts = split
    steps = cap // CHUNK // parts
    lead = which * steps * CHUNK
    smem = pl.BlockSpec(memory_space=pltpu.SMEM)
    hbm = pl.BlockSpec(memory_space=pl.ANY)
    ins, outs, scratch = {}, {}, {}

    def whole(shape):
        zeros = (0,) * len(shape)
        return pl.BlockSpec(shape, lambda c: zeros, pipeline_mode=pl.Buffered(1))

    def take(spec, **arrays):
        for name, array in arrays.items():
            ins[name] = (array, whole(array.shape) if spec is None else spec)

    def take_block(**arrays):
        for name, array in arrays.items():
            at = (index,) + (0,) * (array.ndim - 1)
            spec = pl.BlockSpec((None,) + array.shape[1:], lambda c, at=at: at, pipeline_mode=pl.Buffered(1))
            ins[name] = (array, spec)

    def chunked(shape):
        zeros = (0,) * (len(shape) - 1)
        return pl.BlockSpec(shape, lambda c: (which * steps + c,) + zeros)

    def give(dtype=BF16, **shapes):
        for name, shape in shapes.items():
            outs[name] = (jax.ShapeDtypeStruct(shape, dtype), whole(shape))

    flat = lambda factor: (rows, factor * width)
    stash = dict(
        qkv=flat(3),
        probs=(CHUNK, heads, win, win),
        att=flat(1),
        inverse=flat(1),
        h1=flat(1),
        h2=flat(1),
        act=(rows, hidden),
        slope=(rows, hidden),
        da=flat(1),
        do=flat(1),
        aug=flat(1),
    )

    def carry_in(**arrays):
        for name, array in arrays.items():
            ins[name] = (array, chunked(stash[name]))

    def carry_out(**wanted):
        for name in wanted:
            shape = stash[name]
            full = jax.ShapeDtypeStruct((shape[0] * cap // CHUNK,) + shape[1:], BF16)
            outs[name] = (full, chunked(shape))

    g = given
    take(smem, meta=g.meta, tab=g.tab)
    take(hbm, src=g.src, src_oth=g.src_oth)
    if mixer:
        take(hbm, grad_src=g.grad_src, grad_oth=g.grad_oth)
    if ahead:
        take(hbm, earth_own=g.earth_own, earth_oth=g.earth_oth)
        take(None, shift_one=g.shift_one, shift_two=g.shift_two, down_bias=g.down_bias)
        take(None, entry_own=g.entry_own, entry_oth=g.entry_oth)
        take(None, up_bias_own=g.up_bias_own, up_bias_oth=g.up_bias_oth)
    if ahead or mixer:
        take(None, out_bias=g.out_bias, gain_two=g.gain_two)
        take_block(out_own=g.out_own, out_oth=g.out_oth, up_own=g.up_own, up_oth=g.up_oth)
        take_block(down_own=g.down_own, down_oth=g.down_oth)
    if ahead or attention:
        take(None, gain_one=g.gain_one)
        take_block(in_own=g.in_own, in_oth=g.in_oth)
    if attention:
        take(None, sums_small=g.sums_small, sums_hidden=g.sums_hidden)
        carry_in(qkv=g.qkv, probs=g.probs, h1=g.h1, da=g.da, do=g.do, aug=g.aug)
    elif not ahead:
        carry_in(att=g.att, inverse=g.inverse, h2=g.h2, act=g.act, slope=g.slope)

    half_shape = (half, width)
    if ahead:
        carry_out(qkv=1, probs=1, att=1, h1=1)
        if not mixer:
            carry_out(inverse=1, h2=1, act=1, slope=1)
    if mixer:
        carry_out(da=1, do=1, aug=1)
    if (ahead and not shifted) or (attention and shifted):
        give(out=(cap, 2) + half_shape, out_half=half_shape)
    if (ahead and shifted) or (attention and not shifted):
        give(keep=(cap // parts,) + half_shape, send=(cap // parts,) + half_shape)
    if mixer:
        pack = (padded(2 * hidden_part + width // 2, devices), width)
        give(pack_own=pack, pack_oth=pack)
        give(F32, sums_small=(6, width), sums_hidden=(1, hidden))
    if attention:
        pack = (padded(pack_rows(width, own_heads, win).total, devices), width)
        give(pack_own=pack, pack_oth=pack)

    def hold(dtype=BF16, **shapes):
        for name, shape in shapes.items():
            scratch[name] = pltpu.VMEM(shape, dtype)

    halves = (cap, 2) + half_shape
    hold(xs=halves)
    scratch.update(x_sem=pltpu.SemaphoreType.DMA((cap, 2)))
    if ahead:
        hold(F32, bias=(heads, win, win))
        scratch.update(b_sem=pltpu.SemaphoreType.DMA((2,)))
    if ahead or attention:
        hold(w_in=(3 * width, width))
    if ahead or mixer:
        hold(wo=(width, width))
        hold(I32, lat=(win, 128), col=(win, 128))
    if ahead and mixer:
        hold(inverse=flat(1), h2=flat(1), act=(rows, hidden))
    if mixer:
        hold(rs=halves, rr=flat(1), du=(rows, hidden), spread=(width, width))
        scratch.update(r_sem=pltpu.SemaphoreType.DMA((cap, 2)))
        hold(F32, acc_up=(width, hidden), acc_down=(width, hidden), acc_hidden=(8, hidden), acc_out=(width, width))
    if attention:
        hold(dqkv=flat(3))
        hold(F32, acc_in=(width, 3 * width), acc_earth=(heads, win, win))
        hold(F32, acc_entry=(8, 3 * width))
    if mixer or attention:
        hold(F32, acc_small=(6, 8, width))

    matmuls = cap * win * (4 * width * width + 2 * width * hidden)
    result = pl.pallas_call(
        functools.partial(
            block_kernel, [*ins, *outs, *scratch], stages, index, head_width, (lead, steps * CHUNK)
        ),
        grid=(steps,),
        out_shape=tuple(shape for shape, _ in outs.values()),
        in_specs=[spec for _, spec in ins.values()],
        out_specs=tuple(spec for _, spec in outs.values()),
        scratch_shapes=list(scratch.values()),
        compiler_params=pltpu.CompilerParams(vmem_limit_bytes=VMEM_LIMIT),
        cost_estimate=pl.CostEstimate(
            flops=2 * sum(stages) * matmuls // COST_CUT,
            bytes_accessed=8 * sum(stages) * cap * win * width * 2 // COST_CUT,
            transcendentals=cap * win * hidden // COST_CUT,
        ),
        name=("ahead" if ahead else "") + ("mixer" if mixer else "") + ("attention" if attention else "") + str(index + 1),
    )(*(array for array, _ in ins.values()))
    return Bag(**dict(zip(outs, result, strict=True)))


def settle_kernel(counts, place, *refs):
    refs = list(refs)
    held = [[refs.pop(0) for _ in range(count)] for count in counts]
    out_a, out_b, zeros, sems = refs
    home = place.shape[1]
    zeros[...] = jnp.zeros_like(zeros)

    def start(s, carry):
        for j, out in enumerate((out_a, out_b)):
            source = place[j, s]

            @pl.when(source < 0)
            def _(out=out, j=j):
                pltpu.make_async_copy(zeros, out.at[s], sems.at[j, s]).start()

            low = 0
            for ref in held[j]:
                high = low + ref.shape[0]

                @pl.when((source >= low) & (source < high))
                def _(ref=ref, out=out, j=j, at=source - low):
                    pltpu.make_async_copy(ref.at[at], out.at[s], sems.at[j, s]).start()

                low = high

        return carry

    lax.fori_loop(0, home, start, 0)

    def finish(s, carry):
        for j, out in enumerate((out_a, out_b)):
            pltpu.make_async_copy(zeros, out.at[s], sems.at[j, s]).wait()
        return carry

    lax.fori_loop(0, home, finish, 0)


def settle(place, first, second):
    home = place.shape[1]
    half_shape = first[0].shape[1:]
    hbm = pl.BlockSpec(memory_space=pl.ANY)
    vmem = pl.BlockSpec(memory_space=pltpu.VMEM)
    shape = jax.ShapeDtypeStruct((home,) + half_shape, BF16)
    counts = (len(first), len(second))
    return pl.pallas_call(
        functools.partial(settle_kernel, counts),
        out_shape=(shape, shape),
        in_specs=[pl.BlockSpec(memory_space=pltpu.SMEM)] + [vmem] * sum(counts),
        out_specs=(hbm, hbm),
        scratch_shapes=[pltpu.VMEM(half_shape, BF16), pltpu.SemaphoreType.DMA((2, home))],
        compiler_params=pltpu.CompilerParams(vmem_limit_bytes=VMEM_LIMIT),
        name="settle",
    )(place, *first, *second)


def local_kernel(jobs, digits_ref, *refs):
    refs = list(refs)
    ins = [[refs.pop(0) for _ in range(count)] for _, count, _, _ in jobs]
    outs = [[refs.pop(0) for _ in range(size if scatter else 1)] for scatter, _, size, _ in jobs]
    assert not refs
    for (scatter, _, size, stage), parts, made in zip(jobs, ins, outs):
        digit = digits_ref[stage]
        if scatter:
            rows = made[0].shape[0]
            for k, out in enumerate(made):
                at = pl.multiple_of((digit ^ k) * rows, rows) if size > 1 else 0
                total = parts[0][pl.ds(at, rows), :].astype(F32)
                for part in parts[1:]:
                    total = total + part[pl.ds(at, rows), :].astype(F32)
                out[...] = total.astype(BF16)
        else:
            rows = parts[0].shape[0]
            for k, part in enumerate(parts):
                made[0][pl.ds(pl.multiple_of((digit ^ k) * rows, rows), rows), :] = part[...]


def dp_groups(devices):
    sizes = []
    while devices > 1:
        size = 4 if devices % 4 == 0 else 2
        sizes.append(size)
        devices //= size
    return sizes


def with_peer(value, stride, k):
    devices = lax.axis_size(DP)
    return lax.ppermute(value, DP, [(d, d ^ (k * stride)) for d in range(devices)])


def stack_kernel(counts, *refs):
    out, pairs = refs[-1], refs[:-1]
    at = 0
    for at_pair, (one, other) in enumerate(zip(pairs[0::2], pairs[1::2])):
        rows = counts[at_pair]
        out[at : at + rows, :] = (one[:rows].astype(F32) + other[:rows].astype(F32)).astype(BF16)
        at += rows


def stack(counts, *pairs):
    vmem = pl.BlockSpec(memory_space=pltpu.VMEM)
    return pl.pallas_call(
        functools.partial(stack_kernel, counts),
        out_shape=jax.ShapeDtypeStruct((sum(counts), pairs[0][0].shape[1]), BF16),
        in_specs=[vmem] * (2 * len(pairs)),
        out_specs=vmem,
        compiler_params=pltpu.CompilerParams(vmem_limit_bytes=VMEM_LIMIT),
        name="stack",
    )(*(value for pair in pairs for value in pair))


class DpSum:
    def __init__(self, parts):
        self.parts = parts
        self.phase = 0
        self.stages, stride = [], 1
        for size in dp_groups(lax.axis_size(DP)):
            self.stages.append((size, stride))
            stride *= size

    def job(self):
        count = len(self.stages)
        if self.phase < count:
            return (True, len(self.parts), self.stages[self.phase][0], self.phase)
        if self.phase == count:
            return (True, len(self.parts), 1, 0)
        stage = 2 * count - self.phase
        return (False, len(self.parts), self.stages[stage][0], stage)

    def accept(self, made):
        count = len(self.stages)
        if self.phase < count:
            size, stride = self.stages[self.phase]
            self.parts = [made[0]] + [with_peer(made[k], stride, k) for k in range(1, size)]
        elif self.phase < 2 * count:
            size, stride = self.stages[2 * count - 1 - self.phase]
            self.parts = [made[0]] + [with_peer(made[0], stride, k) for k in range(1, size)]
        else:
            self.parts = made
        self.phase += 1

    def last(self):
        return self.phase >= 2 * len(self.stages)


def advance(sums, digits, *ties):
    sums = [s for s in sums if not s.last()]
    if not sums:
        return ties
    jobs = [s.job() for s in sums]
    inputs, shapes, counts = [], [], []
    for s, (scatter, count, size, _) in zip(sums, jobs):
        rows, width = s.parts[0].shape
        inputs += s.parts
        made = [(rows // size, width)] * size if scatter else [(rows * size, width)]
        shapes += made
        counts.append(len(made))
    smem = pl.BlockSpec(memory_space=pltpu.SMEM)
    vmem = pl.BlockSpec(memory_space=pltpu.VMEM)
    outs = pl.pallas_call(
        functools.partial(local_kernel, jobs),
        out_shape=tuple(jax.ShapeDtypeStruct(shape, BF16) for shape in shapes),
        in_specs=[smem] + [vmem] * len(inputs),
        out_specs=(vmem,) * len(shapes),
        compiler_params=pltpu.CompilerParams(vmem_limit_bytes=VMEM_LIMIT),
        name="fold",
    )(digits, *inputs)
    outs, ties = lax.optimization_barrier((list(outs), ties))
    for s, count in zip(sums, counts):
        s.accept(outs[:count])
        outs = outs[count:]
    return ties


def unpack_kernel(layout, count, digit_ref, *refs):
    refs = list(refs)
    pieces = [[refs.pop(0) for _ in range(count)] for _ in range(2)]
    whole_two = refs.pop(0)
    up, down, inward, out, earth, hidden, entry, *rest_refs = refs
    small, joined = rest_refs[:6], rest_refs[6:]
    digit = digit_ref[0]
    for parts, whole in zip(pieces, joined):
        rows = parts[0].shape[0]
        for k, piece in enumerate(parts):
            whole[pl.ds(pl.multiple_of((digit ^ k) * rows, rows), rows), :] = piece[...]
    width = up.shape[1]
    hidden_part = up.shape[2]
    part = width // 2
    win = earth.shape[2]
    third = win // 3
    split = 2 * hidden_part + part
    packs = [(joined[0], 0, joined[1], 0), (whole_two, 0, whole_two, split)]
    for b, (pack, base, other, base_other) in enumerate(packs):
        for at in range(0, hidden_part, width):
            low = base + at
            up[b, :, at : at + width] = pack[low : low + width, :].astype(F32)
            low += hidden_part
            down[b, at : at + width, :] = pack[low : low + width, :].T.astype(F32)

        def lines_of(place, start, size):
            low = base_other + place + start
            return other[low : low + size, :].astype(F32)

        for j in range(3):
            inward[b, j] = lines_of(layout.inward, j * part, part)
        low = base + 2 * hidden_part
        out[b] = pack[low : low + part, :].astype(F32)
        rest = lines_of(layout.rest, 0, third)
        rest = jnp.concatenate([rest[:, k * 128 : (k + 1) * 128] for k in range(3)], axis=0)
        for k in range(earth.shape[1]):
            main = lines_of(layout.earth, (k // 3) * win, win)
            earth[b, k, :, :128] = main[:, (k % 3) * 128 : (k % 3 + 1) * 128]
            earth[b, k, :, 128:] = rest[:, k * (win - 128) : (k + 1) * (win - 128)]
        lines = lines_of(layout.small, 0, 16)
        for k, table in enumerate(small):
            table[b : b + 1, :] = lines[k : k + 1]
        for j, at in enumerate(range(0, hidden_part, width)):
            hidden[b : b + 1, at : at + width] = lines[6 + j : 7 + j]
        last = lines[6 + hidden_part // width : 7 + hidden_part // width]
        entry[b, 0:1] = last[:, :part]
        entry[b, 1:2] = last[:, part:]


def unpack(digit, hidden_parts, attention_parts, whole_two, width, hidden_part, own_heads, win):
    vmem = pl.BlockSpec(memory_space=pltpu.VMEM)
    shapes = (
        (2, width, hidden_part),
        (2, hidden_part, width),
        (2, 3, width // 2, width),
        (2, width // 2, width),
        (2, own_heads, win, win),
        (2, hidden_part),
        (2, 2, width // 2),
    ) + ((2, width),) * 6
    count = len(hidden_parts)
    return pl.pallas_call(
        functools.partial(unpack_kernel, pack_rows(width, own_heads, win), count),
        out_shape=tuple(jax.ShapeDtypeStruct(shape, F32) for shape in shapes),
        in_specs=[pl.BlockSpec(memory_space=pltpu.SMEM)] + [vmem] * (2 * count + 1),
        out_specs=(vmem,) * len(shapes),
        scratch_shapes=[
            pltpu.VMEM((parts[0].shape[0] * count, width), BF16) for parts in (hidden_parts, attention_parts)
        ],
        compiler_params=pltpu.CompilerParams(vmem_limit_bytes=VMEM_LIMIT),
        name="unpack",
    )(digit, *hidden_parts, *attention_parts, whole_two)


def across(value):
    return lax.ppermute(value, TENSOR, [(0, 1), (1, 0)])


def local(
    tokens,
    token_mask,
    shift_next,
    cotangent,
    attend_gain,
    attend_shift,
    inward_weight,
    inward_bias,
    earth_bias,
    outward_weight,
    outward_bias,
    mixer_gain,
    mixer_shift,
    up_weight,
    up_bias,
    down_weight,
    down_bias,
):
    home, half, width = tokens.shape
    cap = home // 2
    part = lax.axis_index(TENSOR).astype(I32).reshape(1)
    tokens_oth = across(tokens)
    inward = jnp.transpose(inward_weight, (0, 2, 3, 1))
    own_heads = earth_bias.shape[1]
    hidden_part = up_weight.shape[2]
    win = 2 * half
    cotangent_oth = across(cotangent)
    meta, tab, place = make_plan(part, token_mask, shift_next, cap)
    common = dict(
        meta=meta,
        tab=tab,
        gain_one=attend_gain,
        shift_one=attend_shift,
        out_bias=outward_bias,
        gain_two=mixer_gain,
        shift_two=mixer_shift,
        down_bias=down_bias,
        entry_own=inward_bias,
        entry_oth=across(inward_bias),
        up_bias_own=up_bias,
        up_bias_oth=across(up_bias),
        in_own=inward,
        in_oth=across(inward),
        earth_own=earth_bias,
        earth_oth=across(earth_bias),
        out_own=outward_weight,
        out_oth=across(outward_weight),
        up_own=up_weight,
        up_oth=across(up_weight),
        down_own=down_weight,
        down_oth=across(down_weight),
    )
    sizes = (cap, half, width, own_heads, hidden_part)
    devices = lax.axis_size(DP)

    def run(stages, index, *more, split=(0, 1)):
        given = dict(common)
        for group in more:
            given.update(vars(group))
        return run_block(stages, index, Bag(**given), sizes, devices, split)

    rank = lax.axis_index(DP).astype(I32)
    digits, stride = [], 1
    for size in dp_groups(devices):
        digits.append(rank // stride % size)
        stride *= size
    digits = jnp.stack(digits)

    def sum_of(kernel):
        return DpSum([kernel.pack_own, across(kernel.pack_oth)])

    first = Bag(src=tokens, src_oth=tokens_oth)
    ahead_one = run((True, False, False), 0, first)
    second = Bag(src=ahead_one.out, src_oth=across(ahead_one.out_half))
    mixer_two = run((True, True, False), 1, second, Bag(grad_src=cotangent, grad_oth=cotangent_oth))
    pack_far = across(mixer_two.pack_oth)
    recv_b = across(mixer_two.send)
    attention_two = run((False, False, True), 1, mixer_two, second)
    half_far = across(attention_two.out_half)
    filled = (2 * hidden_part + width // 2, pack_rows(width, own_heads, win).total)
    pack_two = stack(filled, (mixer_two.pack_own, pack_far), (attention_two.pack_own, across(attention_two.pack_oth)))
    pack_two, half_far = lax.optimization_barrier((pack_two, half_far))
    sum_two = lax.psum(pack_two, DP)
    back = Bag(grad_src=attention_two.out, grad_oth=half_far)
    mixer_one = run((False, True, False), 0, ahead_one, first, back)
    sum_mixer_one = sum_of(mixer_one)
    (do,) = advance([sum_mixer_one], digits, mixer_one.do)
    halves, across_one = [], []
    for which in range(PARTS):
        if which:
            (do,) = advance([sum_mixer_one], digits, do)
        halves.append(run((False, False, True), 0, ahead_one, mixer_one, Bag(do=do), first, split=(which, PARTS)))
        far, parts = lax.optimization_barrier((halves[-1].pack_oth, sum_mixer_one.parts))
        sum_mixer_one.parts = parts
        across_one.append(across(far))
    sum_attention_one = DpSum([half_of.pack_own for half_of in halves] + across_one)
    recv_a = [across(half_of.send) for half_of in halves]
    sums = [sum_mixer_one, sum_attention_one]
    while not all(s.last() for s in sums):
        advance(sums, digits)
    tokens_grad, block_output = settle(
        place, [half_of.keep for half_of in halves] + recv_a, [mixer_two.keep, recv_b]
    )
    g_up, g_down, g_in, g_out, g_earth, hidden, entry, *small = unpack(
        digits[:1], sum_mixer_one.parts, sum_attention_one.parts, sum_two, width, hidden_part, own_heads, win
    )
    return (
        block_output,
        tokens_grad,
        small[0],
        small[1],
        jnp.transpose(g_in, (0, 3, 1, 2)),
        entry,
        g_earth,
        g_out,
        small[2],
        small[3],
        small[4],
        g_up,
        hidden,
        g_down,
        small[5],
    )


def solution(mesh):
    placed = (
        P(DP, TENSOR, None),
        P(DP, None),
        P(DP),
        P(DP, TENSOR, None),
        P(),
        P(),
        P(None, None, None, TENSOR),
        P(None, None, TENSOR),
        P(None, TENSOR, None, None),
        P(None, TENSOR, None),
        P(),
        P(),
        P(),
        P(None, None, TENSOR),
        P(None, TENSOR),
        P(None, TENSOR, None),
        P(),
    )
    return jax.shard_map(
        local,
        mesh=mesh,
        in_specs=placed,
        out_specs=(
            P(DP, TENSOR, None),
            P(DP, TENSOR, None),
            P(),
            P(),
            P(None, None, None, TENSOR),
            P(None, None, TENSOR),
            P(None, TENSOR, None, None),
            P(None, TENSOR, None),
            P(),
            P(),
            P(),
            P(None, None, TENSOR),
            P(None, TENSOR),
            P(None, TENSOR, None),
            P(),
        ),
        check_vma=False,
    )
```
